256 devices in a mesh: dp: 32 (over y_hi, z, core), tensor: 8 (over x, y_lo).
Axes of the slice: x: 4, y: 4 (y_hi: 2, y_lo: 2; y = y_hi * 2 + y_lo), z: 8, core: 2. Of those that a mesh axis runs over, the one named last changes fastest.
Arguments:
- tokens: bfloat16 [32768, 3072], P(('dp', 'tensor')), may hold values from -40 to 40
- indices: int32 [16384], P(('dp', 'tensor')), may hold values from 0 to 127
- gate_weight: bfloat16 [3072, 8192], P(None, 'tensor'), may hold values from -0.109375 to 0.109375
- up_weight: bfloat16 [3072, 8192], P(None, 'tensor'), may hold values from -0.109375 to 0.109375
Outputs:
- input_factor: float32 [384, 3072], P('dp', 'tensor')
- hidden_factor: float32 [1024, 8192], P('dp', 'tensor')
The draws below stay inside these ranges and needn't reach their ends.
All inputs are finite; a program needn't handle non-finite values.
Results may differ from the reference program's by a relative error of at most 0.0014.
Values may be sent and summed in bfloat16 or wider, within the bound.
A program may use at most 128 MiB of HBM per device.

```python
import math
import jax
import jax.numpy as jnp
from jax import lax

D = 3072
IBLK = 384
HBLK = 1024
SEQ_DEV = 128
SAMP = 64
TOKENS = 32768
SAMPLES = 16384
HID = 8192


def draw_tokens(key, part):
    key = jax.random.fold_in(key, 11)
    row_key, col_key, value_key = jax.random.split(key, 3)
    row_scale = jnp.exp(jax.random.uniform(row_key, (TOKENS, 1), jnp.float32, math.log(0.6), math.log(1.0)))
    col_scale = jnp.exp(jax.random.uniform(col_key, (1, D), jnp.float32, math.log(0.3), math.log(3.0)))
    values_raw = jax.random.normal(value_key, (TOKENS, D), jnp.float32)
    return jnp.clip(values_raw * row_scale * col_scale, -40.0, 40.0).astype(jnp.bfloat16)


def set_ends(array, rng, smallest, top_value):
    spot = [jax.random.randint(jax.random.fold_in(rng, axis), (), 0, length) for axis, length in enumerate(array.shape)]
    longest = array.shape.index(max(array.shape))
    neighbour = spot[:longest] + [(spot[longest] + 1) % array.shape[longest]] + spot[longest + 1:]
    return array.at[tuple(spot)].set(smallest).at[tuple(neighbour)].set(top_value)


def block_scale(key, shape, shards, low, top_value):
    def one(position, parts):
        draws = jax.random.uniform(jax.random.fold_in(jax.random.fold_in(key, 6), position), (parts,), jnp.float32, low / len(shards), top_value / len(shards))
        return jnp.repeat(jnp.exp(draws), shape[position] // parts).reshape((-1,) + (1,) * (len(shape) - position - 1))

    loudness = one(*shards[0])
    for cut in shards[1:]:
        loudness = loudness * one(*cut)
    return loudness


def normal_values(rng, shape, deviation, reach, shards=(), held_as=jnp.bfloat16):
    entries = jax.random.normal(rng, shape, jnp.float32) * deviation
    if len(shards) > 0:
        entries = block_scale(rng, shape, shards, -0.22, 0.18) * entries
    return jnp.clip(entries, min=-reach, max=reach).astype(held_as)


def setup_inputs(seed: int = 0) -> dict:
    keys = jax.random.split(jax.random.key(seed), 5)
    tokens = draw_tokens(jax.random.fold_in(keys[4], 71), 0)
    indices = set_ends(jax.random.randint(keys[1], (SAMPLES,), 0, SEQ_DEV), jax.random.fold_in(keys[1], 1), 0, SEQ_DEV - 1).astype(jnp.int32)
    gate_weight = normal_values(keys[2], (D, HID), D ** -0.5, 0.109375, ((1, 8),))
    up_weight = normal_values(keys[3], (D, HID), D ** -0.5, 0.109375, ((1, 8),))
    return dict(tokens=tokens, indices=indices, gate_weight=gate_weight, up_weight=up_weight)


def gram_blocks(matrix, block):
    stacked = matrix.reshape(matrix.shape[0], matrix.shape[1] // block, block).transpose(1, 0, 2)

    def one_block(piece_rows):
        return jnp.dot(piece_rows.T, piece_rows, preferred_element_type=jnp.float32)

    grams = lax.map(one_block, stacked)
    return grams.transpose(1, 0, 2).reshape(block, matrix.shape[1])


def reference(tokens, indices, gate_weight, up_weight):
    source = jnp.arange(SAMPLES, dtype=jnp.int32) // SAMP
    sampled = jnp.take(tokens, source * SEQ_DEV + indices.astype(jnp.int32), axis=0)
    gate_pre = jnp.dot(sampled, gate_weight, preferred_element_type=jnp.float32)
    up_pre = jnp.dot(sampled, up_weight, preferred_element_type=jnp.float32)
    hidden = (jax.nn.silu(gate_pre) * up_pre).astype(jnp.bfloat16)
    inverse_count = 1.0 / SAMPLES
    input_factor = gram_blocks(sampled, IBLK) * inverse_count
    hidden_factor = gram_blocks(hidden, HBLK) * inverse_count
    return (input_factor, hidden_factor)
```

```python
import jax
import jax.numpy as jnp
from jax import lax
from jax.experimental import pallas as pl
from jax.experimental.pallas import tpu as pltpu
from jax.sharding import PartitionSpec as P

D = 3072
UNITS = 1024
IBLK = 384
SAMP = 64
SEQ = 128
ROWS = 512
CHUNKS = 4
KC = D // CHUNKS
TILE = 256
NT = UNITS // TILE
OWN_ROWS = 32
IN_ROWS = 12
IN_PAD = 16
DZ = (4, 3, 5, 2, 6, 1, 7, 0)
INV = 1.0 / 16384
MESH = pl.DeviceIdType.MESH
F32 = jnp.float32
BF16 = jnp.bfloat16

S_OWN, S_XM, S_XP, S_X2, S_Y, S_YXM, S_YXP, S_YX2 = (64 * i for i in range(8))
MSGS = (
    (S_OWN, S_XM, 0, 64, "xp"),
    (S_OWN, S_XP, 0, 64, "xm"),
    (S_OWN, S_Y, 0, 64, "y"),
    (S_XM, S_X2, 0, 32, "xp"),
    (S_XP, S_X2, 32, 32, "xm"),
    (S_XM, S_YXM, 0, 64, "y"),
    (S_XP, S_YXP, 0, 64, "y"),
    (S_X2, S_YX2, 0, 32, "y"),
    (S_YXM, S_YX2, 32, 16, "xp"),
    (S_YXP, S_YX2, 48, 16, "xm"),
)
NM = len(MSGS)


def kernel(
    idx_ref, tok_hbm, wg_hbm, wu_hbm, oin_ref, oh_ref,
    tok, wg, wu, x, accg, accu, h, hs, sel, hts, g, insel, gin, gin_s, gin_sib,
    gin_y, inz, inz_r, ys, yr, zs, zr,
    tok_sem, w_sem, ag_s, ag_r, h_s, h_r, y_s, y_r, z_s, z_r, in_s, in_r, inz_s, inz_rs,
):
    dp = lax.axis_index("dp")
    t = lax.axis_index("tensor")
    yhi = dp // 16
    z = (dp // 2) % 8
    core = dp % 2
    xx = t // 2
    ylo = t % 2
    yhi_p = yhi + core * (1 - 2 * yhi)
    sib = (dp + 1 - 2 * core, t)
    ypart = (yhi_p * 16 + z * 2 + core, xx * 2 + 1 - ylo)
    yfar = (dp + 16 - 32 * yhi, t)
    where = {
        "xp": (dp, lax.rem(xx + 1, 4) * 2 + ylo),
        "xm": (dp, lax.rem(xx + 3, 4) * 2 + ylo),
        "y": ypart,
    }
    zpeer = [(yhi * 16 + lax.rem(z + d, 8) * 2 + core, t) for d in DZ[:7]]

    tcopy = pltpu.make_async_copy(tok_hbm, tok, tok_sem)
    tcopy.start()
    wcopies = []
    for c in range(CHUNKS):
        rows = pl.ds(c * KC, KC)
        pair = (
            pltpu.make_async_copy(wg_hbm.at[rows, :], wg.at[rows, :], w_sem.at[c, 0]),
            pltpu.make_async_copy(wu_hbm.at[rows, :], wu.at[rows, :], w_sem.at[c, 1]),
        )
        for cp in pair:
            cp.start()
        wcopies.append(pair)

    barrier = pltpu.get_barrier_semaphore()
    peers = [where["xp"], where["xm"], ypart, sib, yfar] + zpeer
    for peer in peers:
        pl.semaphore_signal(barrier, inc=1, device_id=peer, device_id_type=MESH)

    pick = (lax.broadcasted_iota(jnp.int32, (SEQ, SAMP), 0) == idx_ref[...]).astype(BF16)
    tcopy.wait()
    for c in range(CHUNKS):
        x[c, pl.ds(S_OWN, 64), :] = lax.dot_general(
            pick, tok[:, c * KC:(c + 1) * KC], (((0,), (0,)), ((), ())),
            preferred_element_type=F32,
        ).astype(BF16)

    pl.semaphore_wait(barrier, len(peers))

    def message(c, m):
        src, dst, first, n, way = MSGS[m]
        return pltpu.make_async_remote_copy(
            src_ref=x.at[c, pl.ds(src + first, n), :],
            dst_ref=x.at[c, pl.ds(dst + first, n), :],
            send_sem=ag_s.at[c, m],
            recv_sem=ag_r.at[c, m],
            device_id=where[way],
            device_id_type=MESH,
        )

    msgs = [[message(c, m) for m in range(NM)] for c in range(CHUNKS)]

    def first_sends(c):
        for m in (0, 1, 2):
            msgs[c][m].start()

    def forwards(c):
        msgs[c][0].wait_recv()
        msgs[c][3].start()
        msgs[c][5].start()
        msgs[c][1].wait_recv()
        msgs[c][4].start()
        msgs[c][6].start()

    def last_forwards(c):
        msgs[c][3].wait_recv()
        msgs[c][7].start()
        msgs[c][5].wait_recv()
        msgs[c][8].start()
        msgs[c][6].wait_recv()
        msgs[c][9].start()

    def arrived(c):
        for m in (2, 4, 7, 8, 9):
            msgs[c][m].wait_recv()
        for cp in wcopies[c]:
            cp.wait()

    def multiply(c):
        rows = pl.ds(c * KC, KC)

        @pl.loop(0, NT)
        def _(n):
            cols = pl.ds(pl.multiple_of(n * TILE, TILE), TILE)
            pg = jnp.dot(x[c], wg[rows, cols], preferred_element_type=F32)
            pu = jnp.dot(x[c], wu[rows, cols], preferred_element_type=F32)
            if c == 0:
                accg[n] = pg
                accu[n] = pu
            elif c < CHUNKS - 1:
                accg[n] += pg
                accu[n] += pu
            else:
                gate = accg[n] + pg
                up = accu[n] + pu
                h[n] = (gate / (1.0 + jnp.exp(-gate)) * up).astype(BF16)

    for c in range(CHUNKS):
        first_sends(c)

    col = lax.broadcasted_iota(jnp.int32, (OWN_ROWS, UNITS), 1)
    row = lax.broadcasted_iota(jnp.int32, (OWN_ROWS, UNITS), 0)
    icol = lax.broadcasted_iota(jnp.int32, (IN_PAD, IBLK), 1)
    irow = lax.broadcasted_iota(jnp.int32, (IN_PAD, IBLK), 0)
    for r in range(16):
        to_y = (1 - yhi) if r < 8 else yhi
        owner = to_y * 16 + lax.rem(z + DZ[r % 8], 8) * 2
        mine = owner + core
        other = owner + 1 - core
        sel[pl.ds(r * OWN_ROWS, OWN_ROWS), :] = (col - mine * OWN_ROWS == row).astype(BF16)
        keep = irow < IN_ROWS
        insel[pl.ds(r * IN_PAD, IN_PAD), :] = ((icol - mine * IN_ROWS == irow) & keep).astype(BF16)
        insel[pl.ds(256 + r * IN_PAD, IN_PAD), :] = ((icol - other * IN_ROWS == irow) & keep).astype(BF16)

    for s in range(CHUNKS + 2):
        if s < CHUNKS:
            forwards(s)
        if 1 <= s <= CHUNKS:
            last_forwards(s - 1)
        if s >= 2:
            arrived(s - 2)
            if s - 2 < CHUNKS - 1:
                multiply(s - 2)

    xb = x[t // 2, :, pl.ds(pl.multiple_of((t % 2) * IBLK, IBLK), IBLK)]
    xt = lax.dot_general(insel[...], xb, (((1,), (1,)), ((), ())), preferred_element_type=F32).astype(BF16)
    gi = jnp.dot(xt, xb, preferred_element_type=F32)
    gin[...] = gi[:256]
    gin_s[...] = gi[256:]
    in_sib = pltpu.make_async_remote_copy(
        src_ref=gin_s, dst_ref=gin_sib, send_sem=in_s.at[0], recv_sem=in_r.at[0],
        device_id=sib, device_id_type=MESH,
    )
    in_sib.start()

    multiply(CHUNKS - 1)
    hcopies = []
    for n in range(NT):
        cp = pltpu.make_async_remote_copy(
            src_ref=h.at[n], dst_ref=hs.at[n], send_sem=h_s.at[n], recv_sem=h_r.at[n],
            device_id=sib, device_id_type=MESH,
        )
        cp.start()
        hcopies.append(cp)

    in_sib.wait_recv()
    gin[...] += gin_sib[...]
    in_y = pltpu.make_async_remote_copy(
        src_ref=gin.at[pl.ds(0, 128)], dst_ref=gin_y, send_sem=in_s.at[1], recv_sem=in_r.at[1],
        device_id=yfar, device_id_type=MESH,
    )
    in_y.start()

    def selected(src):
        total = jnp.zeros((512, ROWS), F32)
        for n in range(NT):
            total += lax.dot_general(
                sel[:, n * TILE:(n + 1) * TILE], src[n], (((1,), (1,)), ((), ())),
                preferred_element_type=F32,
            )
        return total.astype(BF16)

    hts[0] = selected(h)
    for cp in hcopies:
        cp.wait_recv()
    hts[1] = selected(hs)

    def gram(rows):
        @pl.loop(0, NT)
        def _(n):
            g[n, rows, :] = jnp.dot(hts[0, rows, :], h[n], preferred_element_type=F32) + jnp.dot(
                hts[1, rows, :], hs[n], preferred_element_type=F32
            )

    gram(pl.ds(0, 256))
    ycopies = []
    for r in range(8):
        for n in range(NT):
            ys[r, :, n * TILE:(n + 1) * TILE] = g[n, r * OWN_ROWS:(r + 1) * OWN_ROWS, :]
        cp = pltpu.make_async_remote_copy(
            src_ref=ys.at[r], dst_ref=yr.at[r], send_sem=y_s.at[r], recv_sem=y_r.at[r],
            device_id=yfar, device_id_type=MESH,
        )
        cp.start()
        ycopies.append(cp)
    gram(pl.ds(256, 256))

    in_y.wait_recv()
    inzcopies = []
    for r in range(8):
        inz[r] = gin[pl.ds(128 + r * IN_PAD, IN_PAD), :] + gin_y[pl.ds(r * IN_PAD, IN_PAD), :]
        if r < 7:
            cp = pltpu.make_async_remote_copy(
                src_ref=inz.at[r], dst_ref=inz_r.at[r], send_sem=inz_s.at[r], recv_sem=inz_rs.at[r],
                device_id=zpeer[r], device_id_type=MESH,
            )
            cp.start()
            inzcopies.append(cp)

    zcopies = []
    for r in range(8):
        ycopies[r].wait_recv()
        for n in range(NT):
            cols = slice(n * TILE, (n + 1) * TILE)
            zs[r, :, cols] = g[n, 256 + r * OWN_ROWS:256 + (r + 1) * OWN_ROWS, :] + yr[r, :, cols]
        if r < 7:
            cp = pltpu.make_async_remote_copy(
                src_ref=zs.at[r], dst_ref=zr.at[r], send_sem=z_s.at[r], recv_sem=z_r.at[r],
                device_id=zpeer[r], device_id_type=MESH,
            )
            cp.start()
            zcopies.append(cp)

    total = inz[7]
    for r in range(7):
        inzcopies[r].wait_recv()
        total += inz_r[r]
    oin_ref[...] = total[:IN_ROWS] * INV

    total = zs[7]
    for r in range(7):
        zcopies[r].wait_recv()
        total += zr[r]
    oh_ref[...] = total * INV

    for c in range(CHUNKS):
        for m in range(NM):
            msgs[c][m].wait_send()
    for cp in hcopies + ycopies + zcopies + inzcopies + [in_sib, in_y]:
        cp.wait_send()


def local(tokens, indices, gate_weight, up_weight):
    vmem = pltpu.VMEM
    dma = pltpu.SemaphoreType.DMA
    return pl.pallas_call(
        kernel,
        out_shape=(
            jax.ShapeDtypeStruct((IN_ROWS, IBLK), F32),
            jax.ShapeDtypeStruct((OWN_ROWS, UNITS), F32),
        ),
        in_specs=[pl.BlockSpec(memory_space=vmem)] + [pl.BlockSpec(memory_space=pl.ANY)] * 3,
        out_specs=[pl.BlockSpec(memory_space=vmem)] * 2,
        scratch_shapes=[
            vmem((SEQ, D), BF16),
            vmem((D, UNITS), BF16),
            vmem((D, UNITS), BF16),
            vmem((CHUNKS, ROWS, KC), BF16),
            vmem((NT, ROWS, TILE), F32),
            vmem((NT, ROWS, TILE), F32),
            vmem((NT, ROWS, TILE), BF16),
            vmem((NT, ROWS, TILE), BF16),
            vmem((512, UNITS), BF16),
            vmem((2, 512, ROWS), BF16),
            vmem((NT, 512, TILE), F32),
            vmem((512, IBLK), BF16),
            vmem((256, IBLK), F32),
            vmem((256, IBLK), F32),
            vmem((256, IBLK), F32),
            vmem((128, IBLK), F32),
            vmem((8, IN_PAD, IBLK), F32),
            vmem((7, IN_PAD, IBLK), F32),
            vmem((8, OWN_ROWS, UNITS), F32),
            vmem((8, OWN_ROWS, UNITS), F32),
            vmem((8, OWN_ROWS, UNITS), F32),
            vmem((7, OWN_ROWS, UNITS), F32),
            dma,
            dma((CHUNKS, 2)),
            dma((CHUNKS, NM)),
            dma((CHUNKS, NM)),
            dma((NT,)),
            dma((NT,)),
            dma((8,)),
            dma((8,)),
            dma((7,)),
            dma((7,)),
            dma((2,)),
            dma((2,)),
            dma((7,)),
            dma((7,)),
        ],
        compiler_params=pltpu.CompilerParams(
            collective_id=0, has_side_effects=True, vmem_limit_bytes=56 * 2**20
        ),
    )(indices.reshape(1, SAMP), tokens, gate_weight, up_weight)


def solution(mesh):
    in_specs = (
        P(("dp", "tensor"), None),
        P(("dp", "tensor")),
        P(None, "tensor"),
        P(None, "tensor"),
    )
    out_specs = (P("dp", "tensor"), P("dp", "tensor"))
    return jax.shard_map(local, mesh=mesh, in_specs=in_specs, out_specs=out_specs, check_vma=False)
```

```python
import jax
import jax.numpy as jnp
from jax import lax
from jax.experimental import pallas as pl
from jax.experimental.pallas import tpu as pltpu
from jax.sharding import PartitionSpec as P

D = 3072
UNITS = 1024
IBLK = 384
SAMP = 64
SEQ = 128
ROWS = 512
CHUNKS = 4
KC = D // CHUNKS
TILE = 256
NT = UNITS // TILE
OWN_ROWS = 32
IN_ROWS = 12
IN_PAD = 16
DZ = (4, 3, 5, 2, 6, 1, 7, 0)
INV = 1.0 / 16384
STEPS = 32000.0
MESH = pl.DeviceIdType.MESH
F32 = jnp.float32
BF16 = jnp.bfloat16
I16 = jnp.int16
I32 = jnp.int32

S_OWN, S_XM, S_XP, S_X2, S_Y, S_YXM, S_YXP, S_YX2 = (64 * i for i in range(8))
MSGS = (
    (S_OWN, S_XM, 0, 64, "xp"),
    (S_OWN, S_XP, 0, 64, "xm"),
    (S_OWN, S_Y, 0, 64, "y"),
    (S_XM, S_X2, 0, 32, "xp"),
    (S_XP, S_X2, 32, 32, "xm"),
    (S_XM, S_YXM, 0, 64, "y"),
    (S_XP, S_YXP, 0, 64, "y"),
    (S_X2, S_YX2, 0, 32, "y"),
    (S_YXM, S_YX2, 32, 16, "xp"),
    (S_YXP, S_YX2, 48, 16, "xm"),
)
NM = len(MSGS)


def row_code(vals):
    top = jnp.max(jnp.abs(vals), axis=1, keepdims=True)
    code = jnp.ceil(8.0 * jnp.log2(jnp.maximum(top, 1e-30)))
    q = jnp.round(vals * (jnp.exp2(code * -0.125) * STEPS))
    return q.astype(I32).astype(I16), code.astype(I32)


def row_scale(code):
    return jnp.exp2(code.astype(I32).astype(F32) * 0.125) * (1.0 / STEPS)


def kernel(
    idx_hbm, tok_hbm, wg_hbm, wu_hbm, oin_ref, oh_ref,
    idx, tok, wg, wu, x, accg, accu, h, hs, hts, g, gin, gin_s, gin_sib,
    iys, iyr, izs, izr, ys, yr, zs, zr,
    tok_sem, w_sem, ag_s, ag_r, h_s, h_r, y_s, y_r, z_s, z_r, in_s, in_r, iz_s, iz_r, rel,
):
    dp = lax.axis_index("dp")
    t = lax.axis_index("tensor")
    yhi = dp // 16
    z = (dp // 2) % 8
    core = dp % 2
    xx = t // 2
    ylo = t % 2
    yhi_p = yhi + core * (1 - 2 * yhi)
    sib = (dp + 1 - 2 * core, t)
    ypart = (yhi_p * 16 + z * 2 + core, xx * 2 + 1 - ylo)
    yfar = (dp + 16 - 32 * yhi, t)
    where = {
        "xp": (dp, lax.rem(xx + 1, 4) * 2 + ylo),
        "xm": (dp, lax.rem(xx + 3, 4) * 2 + ylo),
        "y": ypart,
    }

    def zpeer(d):
        return (yhi * 16 + lax.rem(z + d, 8) * 2 + core, t)

    icopy = pltpu.make_async_copy(idx_hbm, idx, tok_sem.at[0])
    icopy.start()
    tcopy = pltpu.make_async_copy(tok_hbm, tok, tok_sem.at[1])
    tcopy.start()

    barrier = pltpu.get_barrier_semaphore()
    peers = [where["xp"], where["xm"], ypart, sib, yfar, zpeer(1), zpeer(7)]
    for peer in peers:
        pl.semaphore_signal(barrier, inc=1, device_id=peer, device_id_type=MESH)

    def wcopy(c):
        rows = pl.ds(pl.multiple_of(c * KC, KC), KC)
        return (
            pltpu.make_async_copy(wg_hbm.at[rows, :], wg.at[rows, :], w_sem.at[c, 0]),
            pltpu.make_async_copy(wu_hbm.at[rows, :], wu.at[rows, :], w_sem.at[c, 1]),
        )

    icopy.wait()
    pick = (lax.broadcasted_iota(I32, (SEQ, SAMP), 0) == idx[...]).astype(BF16)
    tcopy.wait()
    for c in range(CHUNKS):
        x[c, pl.ds(S_OWN, 64), :] = lax.dot_general(
            pick, tok[:, c * KC:(c + 1) * KC], (((0,), (0,)), ((), ())),
            preferred_element_type=F32,
        ).astype(BF16)
    for c in range(CHUNKS):
        for cp in wcopy(c):
            cp.start()

    pl.semaphore_wait(barrier, len(peers))

    def message(c, m):
        src, dst, first, n, way = MSGS[m]
        return pltpu.make_async_remote_copy(
            src_ref=x.at[c, pl.ds(src + first, n), :],
            dst_ref=x.at[c, pl.ds(dst + first, n), :],
            send_sem=ag_s.at[c, m],
            recv_sem=ag_r.at[c, m],
            device_id=where[way],
            device_id_type=MESH,
        )

    def tell(k):
        pl.semaphore_signal(rel.at[k, 0], inc=1, device_id=zpeer(1), device_id_type=MESH)
        pl.semaphore_signal(rel.at[k, 1], inc=1, device_id=zpeer(7), device_id_type=MESH)

    def told(k):
        pl.semaphore_wait(rel.at[k, 0], 1)
        pl.semaphore_wait(rel.at[k, 1], 1)

    def forwards(c):
        message(c, 0).wait_recv()
        message(c, 3).start()
        message(c, 5).start()
        message(c, 1).wait_recv()
        message(c, 4).start()
        message(c, 6).start()

    def last_forwards(c):
        message(c, 3).wait_recv()
        message(c, 7).start()
        message(c, 5).wait_recv()
        message(c, 8).start()
        message(c, 6).wait_recv()
        message(c, 9).start()

    def arrived(c):
        for m in (2, 4, 7, 8, 9):
            message(c, m).wait_recv()
        for cp in wcopy(c):
            cp.wait()

    def products(c, n):
        rows = pl.ds(pl.multiple_of(c * KC, KC), KC)
        cols = pl.ds(pl.multiple_of(n * TILE, TILE), TILE)
        pg = jnp.dot(x[c], wg[rows, cols], preferred_element_type=F32)
        pu = jnp.dot(x[c], wu[rows, cols], preferred_element_type=F32)
        return pg, pu

    for c in range(CHUNKS):
        for m in (0, 1, 2):
            message(c, m).start()
    tell(0)

    accg[...] = jnp.zeros_like(accg)
    accu[...] = jnp.zeros_like(accu)

    forwards(0)
    told(0)
    tell(1)
    forwards(1)
    last_forwards(0)
    told(1)
    tell(2)

    @pl.loop(0, CHUNKS - 1)
    def _(c):
        @pl.when(c < CHUNKS - 2)
        def _():
            forwards(c + 2)

        last_forwards(c + 1)
        arrived(c)

        @pl.loop(0, NT)
        def _(n):
            pg, pu = products(c, n)
            accg[n] += pg
            accu[n] += pu

    told(2)
    arrived(CHUNKS - 1)

    icol = lax.broadcasted_iota(I32, (IN_PAD, IBLK), 1)
    irow = lax.broadcasted_iota(I32, (IN_PAD, IBLK), 0)

    def in_rows(which):
        parts = []
        for r in range(16):
            to_y = (1 - yhi) if r < 8 else yhi
            owner = to_y * 16 + lax.rem(z + DZ[r % 8], 8) * 2 + which
            parts.append(((icol - owner * IN_ROWS == irow) & (irow < IN_ROWS)).astype(BF16))
        return jnp.concatenate(parts, axis=0)

    xb = x[t // 2, :, pl.ds(pl.multiple_of((t % 2) * IBLK, IBLK), IBLK)]
    for which, dst in ((1 - core, gin_s), (core, gin)):
        xt = lax.dot_general(
            in_rows(which), xb, (((1,), (1,)), ((), ())), preferred_element_type=F32
        ).astype(BF16)
        dst[...] = jnp.dot(xt, xb, preferred_element_type=F32)
    in_sib = pltpu.make_async_remote_copy(
        src_ref=gin_s, dst_ref=gin_sib, send_sem=in_s.at[0], recv_sem=in_r.at[0],
        device_id=sib, device_id_type=MESH,
    )
    in_sib.start()

    def hcopy(n):
        return pltpu.make_async_remote_copy(
            src_ref=h.at[n], dst_ref=hs.at[n], send_sem=h_s.at[n], recv_sem=h_r.at[n],
            device_id=sib, device_id_type=MESH,
        )

    @pl.loop(0, NT)
    def _(n):
        pg, pu = products(CHUNKS - 1, n)
        gate = accg[n] + pg
        up = accu[n] + pu
        h[n] = (gate / (1.0 + jnp.exp(-gate)) * up).astype(BF16)
        hcopy(n).start()

    scol = lax.broadcasted_iota(I32, (128, TILE), 1)
    srow = lax.broadcasted_iota(I32, (128, TILE), 0)
    pick_rows = (scol == (srow // 32) * 64 + core * 32 + srow % 32).astype(BF16)

    def take_rows(src, n, k):
        rows = lax.dot_general(
            pick_rows, src[n], (((1,), (1,)), ((), ())), preferred_element_type=F32
        ).astype(BF16)
        for q in range(4):
            dz = lax.rem((n % 2) * 4 + q + 8 - z, 8)
            place = jnp.where(dz >= 4, 2 * (dz - 4), 7 - 2 * dz)
            place = place + jnp.where(n // 2 == yhi, 8, 0)
            hts[k, pl.ds(pl.multiple_of(place * 32, 32), 32), :] = rows[q * 32:(q + 1) * 32]

    @pl.loop(0, NT)
    def _(n):
        take_rows(h, n, 0)

    @pl.loop(0, NT)
    def _(n):
        g[n] = jnp.dot(hts[0], h[n], preferred_element_type=F32)

    in_sib.wait_recv()
    q, code = row_code(gin[0:128, :] + gin_sib[0:128, :])
    lane = lax.broadcasted_iota(I32, (16, 128), 1)
    packed = jnp.zeros((16, 128), I32)
    for r in range(8):
        for b in range(3):
            iys[3 * r + b] = q[16 * r:16 * r + 16, 128 * b:128 * b + 128]
        packed = jnp.where(lane // 16 == r, code[16 * r:16 * r + 16], packed)
    iys[24] = packed.astype(I16)
    in_y = pltpu.make_async_remote_copy(
        src_ref=iys, dst_ref=iyr, send_sem=in_s.at[1], recv_sem=in_r.at[1],
        device_id=yfar, device_id_type=MESH,
    )
    in_y.start()

    @pl.loop(0, NT)
    def _(n):
        hcopy(n).wait_recv()
        take_rows(hs, n, 1)

    def add_gram(first):
        @pl.loop(0, NT)
        def _(n):
            rows = pl.ds(first, 256)
            g[n, rows, :] += jnp.dot(hts[1, rows, :], hs[n], preferred_element_type=F32)

    def encode(halves, buf):
        codes = []
        for a, vals in enumerate(halves):
            q, code = row_code(vals)
            for b in range(8):
                buf[8 * a + b] = q[:, 128 * b:128 * b + 128]
            codes.append(code)
        buf[16] = jnp.where(lane < 64, codes[0], codes[1]).astype(I16)

    def decode(buf):
        codes = buf[16]
        out = []
        for a in range(2):
            s = row_scale(codes[:, 64 * a:64 * a + 1])
            cat = jnp.concatenate([buf[8 * a + b] for b in range(8)], axis=1)
            out.append(cat.astype(I32).astype(F32) * s)
        return out

    def g_halves(first):
        out = []
        for a in range(2):
            rows = pl.ds(pl.multiple_of(first + 16 * a, 16), 16)
            out.append(jnp.concatenate([g[n, rows, :] for n in range(NT)], axis=1))
        return out

    def ycopy(r):
        return pltpu.make_async_remote_copy(
            src_ref=ys.at[r], dst_ref=yr.at[r], send_sem=y_s.at[r], recv_sem=y_r.at[r],
            device_id=yfar, device_id_type=MESH,
        )

    def far(r):
        k = (r + 1) // 2
        return zpeer(jnp.where(r % 2 == 0, 4 + k, 4 - k))

    def zcopy(r):
        return pltpu.make_async_remote_copy(
            src_ref=zs.at[r], dst_ref=zr.at[r], send_sem=z_s.at[r], recv_sem=z_r.at[r],
            device_id=far(r), device_id_type=MESH,
        )

    def izcopy(r):
        return pltpu.make_async_remote_copy(
            src_ref=izs.at[r], dst_ref=izr.at[r], send_sem=iz_s.at[r], recv_sem=iz_r.at[r],
            device_id=far(r), device_id_type=MESH,
        )

    add_gram(0)

    @pl.loop(0, 8)
    def _(r):
        encode(g_halves(r * 32), ys.at[r])
        ycopy(r).start()

    add_gram(256)

    in_y.wait_recv()
    codes = iyr[24]
    own_in = None
    for r in range(8):
        s = row_scale(codes[:, 16 * r:16 * r + 1])
        rows = pl.ds(128 + 16 * r, 16)
        cat = jnp.concatenate([iyr[3 * r + b] for b in range(3)], axis=1)
        total = gin[rows, :] + gin_sib[rows, :] + cat.astype(I32).astype(F32) * s
        if r < 7:
            q, code = row_code(total)
            for b in range(3):
                izs[r, b] = q[:, 128 * b:128 * b + 128]
            izs[r, 3] = jnp.broadcast_to(code, (16, 128)).astype(I16)
            izcopy(r).start()
        else:
            gin[pl.ds(0, 16), :] = total

    @pl.loop(0, 7)
    def _(r):
        ycopy(r).wait_recv()
        own = g_halves(256 + r * 32)
        got = decode(yr.at[r])
        encode([a + b for a, b in zip(own, got)], zs.at[r])
        zcopy(r).start()

    ycopy(7).wait_recv()
    own = g_halves(256 + 7 * 32)
    got = decode(yr.at[7])
    for a in range(2):
        oh_ref[pl.ds(16 * a, 16), :] = own[a] + got[a]

    total = gin[pl.ds(0, 16), :]
    for r in range(7):
        izcopy(r).wait_recv()
        s = row_scale(izr[r, 3][:, 0:1])
        cat = jnp.concatenate([izr[r, b] for b in range(3)], axis=1)
        total += cat.astype(I32).astype(F32) * s
    oin_ref[...] = total[:IN_ROWS] * INV

    @pl.loop(0, 7)
    def _(r):
        zcopy(r).wait_recv()
        got = decode(zr.at[r])
        last = jnp.where(r == 6, INV, 1.0)
        for a in range(2):
            rows = pl.ds(16 * a, 16)
            oh_ref[rows, :] = (oh_ref[rows, :] + got[a]) * last

    @pl.loop(0, CHUNKS)
    def _(c):
        for m in range(NM):
            message(c, m).wait_send()

    @pl.loop(0, NT)
    def _(n):
        hcopy(n).wait_send()

    @pl.loop(0, 7)
    def _(r):
        ycopy(r).wait_send()
        zcopy(r).wait_send()
        izcopy(r).wait_send()

    ycopy(7).wait_send()
    in_sib.wait_send()
    in_y.wait_send()


def pass_on(a_ref, b_ref, c_ref, d_ref, sem):
    copies = [
        pltpu.make_async_copy(a_ref, c_ref, sem.at[0]),
        pltpu.make_async_copy(b_ref, d_ref, sem.at[1]),
    ]
    for cp in copies:
        cp.start()
    for cp in copies:
        cp.wait()


def local(tokens, indices, gate_weight, up_weight):
    vmem = pltpu.VMEM
    dma = pltpu.SemaphoreType.DMA
    whole = pl.BlockSpec(memory_space=pl.ANY)
    out_shape = (
        jax.ShapeDtypeStruct((IN_ROWS, IBLK), F32),
        jax.ShapeDtypeStruct((OWN_ROWS, UNITS), F32),
    )
    factors = pl.pallas_call(
        kernel,
        out_shape=out_shape,
        in_specs=[whole] * 4,
        out_specs=[pl.BlockSpec(memory_space=vmem)] * 2,
        scratch_shapes=[
            vmem((1, SAMP), I32),
            vmem((SEQ, D), BF16),
            vmem((D, UNITS), BF16),
            vmem((D, UNITS), BF16),
            vmem((CHUNKS, ROWS, KC), BF16),
            vmem((NT, ROWS, TILE), F32),
            vmem((NT, ROWS, TILE), F32),
            vmem((NT, ROWS, TILE), BF16),
            vmem((NT, ROWS, TILE), BF16),
            vmem((2, 512, ROWS), BF16),
            vmem((NT, 512, TILE), F32),
            vmem((256, IBLK), F32),
            vmem((256, IBLK), F32),
            vmem((256, IBLK), F32),
            vmem((25, 16, 128), I16),
            vmem((25, 16, 128), I16),
            vmem((7, 4, 16, 128), I16),
            vmem((7, 4, 16, 128), I16),
            vmem((8, 17, 16, 128), I16),
            vmem((8, 17, 16, 128), I16),
            vmem((7, 17, 16, 128), I16),
            vmem((7, 17, 16, 128), I16),
            dma((2,)),
            dma((CHUNKS, 2)),
            dma((CHUNKS, NM)),
            dma((CHUNKS, NM)),
            dma((NT,)),
            dma((NT,)),
            dma((8,)),
            dma((8,)),
            dma((7,)),
            dma((7,)),
            dma((2,)),
            dma((2,)),
            dma((7,)),
            dma((7,)),
            pltpu.SemaphoreType.REGULAR((3, 2)),
        ],
        compiler_params=pltpu.CompilerParams(
            collective_id=0, has_side_effects=True, vmem_limit_bytes=56 * 2**20
        ),
    )(indices.reshape(1, SAMP), tokens, gate_weight, up_weight)
    return pl.pallas_call(
        pass_on,
        out_shape=out_shape,
        in_specs=[whole] * 2,
        out_specs=[whole] * 2,
        scratch_shapes=[dma((2,))],
    )(*factors)


def solution(mesh):
    in_specs = (
        P(("dp", "tensor"), None),
        P(("dp", "tensor")),
        P(None, "tensor"),
        P(None, "tensor"),
    )
    out_specs = (P("dp", "tensor"), P("dp", "tensor"))
    return jax.shard_map(local, mesh=mesh, in_specs=in_specs, out_specs=out_specs, check_vma=False)
```

```python
import jax
import jax.numpy as jnp
from jax import lax
from jax.experimental import pallas as pl
from jax.experimental.pallas import tpu as pltpu
from jax.sharding import PartitionSpec as P

D = 3072
UNITS = 1024
IBLK = 384
SAMP = 64
SEQ = 128
ROWS = 512
CHUNKS = 4
KC = D // CHUNKS
TILE = 512
NT = UNITS // TILE
TURN = 256
OWN_ROWS = 32
IN_ROWS = 12
IN_PAD = 16
DZ = (4, 3, 5, 2, 6, 1, 7, 0)
STEP = (1, 3, 7, 2, 6, 1, 7)
INV = 1.0 / 16384
STEPS = 32000.0
MESH = pl.DeviceIdType.MESH
F32 = jnp.float32
BF16 = jnp.bfloat16
I16 = jnp.int16
I32 = jnp.int32

S_OWN, S_XM, S_XP, S_Y, S_YXM, S_YXP, S_X2, S_YX2 = (64 * i for i in range(8))
HALF = 256
MSGS = (
    (S_OWN, S_XM, 0, 64, "xp"),
    (S_OWN, S_XP, 0, 64, "xm"),
    (S_OWN, S_Y, 0, 64, "y"),
    (S_XM, S_X2, 0, 32, "xp"),
    (S_XP, S_X2, 32, 32, "xm"),
    (S_XM, S_YXM, 0, 64, "y"),
    (S_XP, S_YXP, 0, 64, "y"),
    (S_X2, S_YX2, 0, 32, "y"),
    (S_YXM, S_YX2, 32, 16, "xp"),
    (S_YXP, S_YX2, 48, 16, "xm"),
)
NM = len(MSGS)


def row_code(vals):
    top = jnp.max(jnp.abs(vals), axis=1, keepdims=True)
    code = jnp.ceil(8.0 * jnp.log2(jnp.maximum(top, 1e-30)))
    q = jnp.round(vals * (jnp.exp2(code * -0.125) * STEPS))
    return q.astype(I32).astype(I16), code.astype(I32)


def row_scale(code):
    return jnp.exp2(code.astype(I32).astype(F32) * 0.125) * (1.0 / STEPS)


def kernel(
    idx_hbm, tok_hbm, wg_hbm, wu_hbm, oin_ref, oh_ref,
    idx, tok, wg, wu, x, accg, accu, h1, h2, ht1, ht2, g, insel, gin, gin_sib,
    iys, iyr, izs, izr, ys, yr, fs, fr, zs, zr,
    tok_sem, w_sem, ag_s, ag_r, h_s, h_r, y_s, y_r, f_s, f_r, z_s, z_r, in_s, in_r, iz_s, iz_r, rel,
):
    dp = lax.axis_index("dp")
    t = lax.axis_index("tensor")
    yhi = dp // 16
    z = (dp // 2) % 8
    core = dp % 2
    xx = t // 2
    ylo = t % 2
    yhi_p = yhi + core * (1 - 2 * yhi)
    sib = (dp + 1 - 2 * core, t)
    ypart = (yhi_p * 16 + z * 2 + core, xx * 2 + 1 - ylo)
    yfar = (dp + 16 - 32 * yhi, t)
    where = {
        "xp": (dp, lax.rem(xx + 1, 4) * 2 + ylo),
        "xm": (dp, lax.rem(xx + 3, 4) * 2 + ylo),
        "y": ypart,
    }

    def zpeer(d):
        return (yhi * 16 + lax.rem(z + d, 8) * 2 + core, t)

    icopy = pltpu.make_async_copy(idx_hbm, idx, tok_sem.at[0])
    icopy.start()
    tcopy = pltpu.make_async_copy(tok_hbm, tok, tok_sem.at[1])
    tcopy.start()

    barrier = pltpu.get_barrier_semaphore()
    peers = [where["xp"], where["xm"], ypart, sib, yfar, zpeer(1), zpeer(7)]
    for peer in peers:
        pl.semaphore_signal(barrier, inc=1, device_id=peer, device_id_type=MESH)

    def wcopy(c):
        rows = pl.ds(pl.multiple_of(c * KC, KC), KC)
        return (
            pltpu.make_async_copy(wg_hbm.at[rows, :], wg.at[rows, :], w_sem.at[c, 0]),
            pltpu.make_async_copy(wu_hbm.at[rows, :], wu.at[rows, :], w_sem.at[c, 1]),
        )

    icopy.wait()
    pick = (lax.broadcasted_iota(I32, (SEQ, SAMP), 0) == idx[...]).astype(BF16)
    tcopy.wait()
    for c in range(CHUNKS):
        x[c, pl.ds(S_OWN, 64), :] = lax.dot_general(
            pick, tok[:, c * KC:(c + 1) * KC], (((0,), (0,)), ((), ())),
            preferred_element_type=F32,
        ).astype(BF16)
    for c in range(CHUNKS):
        for cp in wcopy(c):
            cp.start()

    pl.semaphore_wait(barrier, len(peers))

    def message(c, m):
        src, dst, first, n, way = MSGS[m]
        return pltpu.make_async_remote_copy(
            src_ref=x.at[c, pl.ds(src + first, n), :],
            dst_ref=x.at[c, pl.ds(dst + first, n), :],
            send_sem=ag_s.at[c, m],
            recv_sem=ag_r.at[c, m],
            device_id=where[way],
            device_id_type=MESH,
        )

    def tell(k):
        pl.semaphore_signal(rel.at[k, 0], inc=1, device_id=zpeer(1), device_id_type=MESH)
        pl.semaphore_signal(rel.at[k, 1], inc=1, device_id=zpeer(7), device_id_type=MESH)

    def told(k):
        pl.semaphore_wait(rel.at[k, 0], 1)
        pl.semaphore_wait(rel.at[k, 1], 1)

    def forwards(c):
        message(c, 0).wait_recv()
        message(c, 3).start()
        message(c, 5).start()
        message(c, 1).wait_recv()
        message(c, 4).start()
        message(c, 6).start()

    def last_forwards(c):
        message(c, 3).wait_recv()
        message(c, 7).start()
        message(c, 5).wait_recv()
        message(c, 8).start()
        message(c, 6).wait_recv()
        message(c, 9).start()

    def products(c, group):
        mine = pl.ds(group * HALF, HALF)
        rows = pl.ds(pl.multiple_of(c * KC, KC), KC)

        @pl.loop(0, NT)
        def _(n):
            cols = pl.ds(pl.multiple_of(n * TILE, TILE), TILE)
            accg[n, mine, :] += jnp.dot(x[c, mine, :], wg[rows, cols], preferred_element_type=F32)
            accu[n, mine, :] += jnp.dot(x[c, mine, :], wu[rows, cols], preferred_element_type=F32)

    hidden = (h1, h2)
    turned = (ht1, ht2)

    def hcopy(group, n):
        ref = hidden[group]
        cols = pl.ds(pl.multiple_of(n * TILE, TILE), TILE)
        return pltpu.make_async_remote_copy(
            src_ref=ref.at[pl.ds(0, HALF), cols], dst_ref=ref.at[pl.ds(HALF, HALF), cols],
            send_sem=h_s.at[group, n], recv_sem=h_r.at[group, n],
            device_id=sib, device_id_type=MESH,
        )

    def finish(group):
        mine = pl.ds(group * HALF, HALF)
        rows = pl.ds((CHUNKS - 1) * KC, KC)

        @pl.loop(0, NT)
        def _(n):
            cols = pl.ds(pl.multiple_of(n * TILE, TILE), TILE)
            last = x[CHUNKS - 1, mine, :]
            gate = accg[n, mine, :] + jnp.dot(last, wg[rows, cols], preferred_element_type=F32)
            up = accu[n, mine, :] + jnp.dot(last, wu[rows, cols], preferred_element_type=F32)
            hidden[group][pl.ds(0, HALF), cols] = (gate / (1.0 + jnp.exp(-gate)) * up).astype(BF16)
            hcopy(group, n).start()

    scol = lax.broadcasted_iota(I32, (128, TURN), 1)
    srow = lax.broadcasted_iota(I32, (128, TURN), 0)
    pick_rows = (scol == (srow // 32) * 64 + core * 32 + srow % 32).astype(BF16)

    def take_rows(group, first, count):
        src = pl.ds(first, count)

        for n in range(UNITS // TURN):
            rows = lax.dot_general(
                pick_rows, hidden[group][src, n * TURN:(n + 1) * TURN], (((1,), (1,)), ((), ())),
                preferred_element_type=F32,
            ).astype(BF16)
            for q in range(4):
                dz = lax.rem((n % 2) * 4 + q + 8 - z, 8)
                place = jnp.where(dz >= 4, 2 * (dz - 4), 7 - 2 * dz)
                place = place + jnp.where(n // 2 == yhi, 8, 0)
                to = pl.ds(pl.multiple_of(place * 32, 32), 32)
                turned[group][to, src] = rows[q * 32:(q + 1) * 32]

    def gram(group, out, first, count):
        rows = pl.ds(out[0], out[1])
        src = pl.ds(first, count)

        @pl.loop(0, NT)
        def _(n):
            cols = pl.ds(pl.multiple_of(n * TILE, TILE), TILE)
            part = jnp.dot(turned[group][rows, src], hidden[group][src, cols], preferred_element_type=F32)
            if group == 0:
                g[n, rows, :] = part
            else:
                g[n, rows, :] += part

    for c in range(CHUNKS):
        for m in (0, 1, 2):
            message(c, m).start()
    tell(0)

    accg[...] = jnp.zeros_like(accg)
    accu[...] = jnp.zeros_like(accu)

    icol = lax.broadcasted_iota(I32, (IN_PAD, IBLK), 1)
    irow = lax.broadcasted_iota(I32, (IN_PAD, IBLK), 0)
    for r in range(32):
        to_y = (1 - yhi) if r % 16 < 8 else yhi
        to_core = core if r < 16 else 1 - core
        owner = to_y * 16 + lax.rem(z + DZ[r % 8], 8) * 2 + to_core
        block = (icol - owner * IN_ROWS == irow) & (irow < IN_ROWS)
        insel[pl.ds(r * IN_PAD, IN_PAD), :] = block.astype(BF16)

    def in_gram(group):
        xb = x[
            t // 2, pl.ds(group * HALF, HALF), pl.ds(pl.multiple_of((t % 2) * IBLK, IBLK), IBLK)
        ]
        xt = lax.dot_general(
            insel[...], xb, (((1,), (1,)), ((), ())), preferred_element_type=F32
        ).astype(BF16)
        part = jnp.dot(xt, xb, preferred_element_type=F32)
        if group == 0:
            gin[...] = part
        else:
            gin[...] += part

    @pl.loop(0, CHUNKS)
    def _(c):
        forwards(c)

        @pl.when(c == 0)
        def _():
            told(0)
            tell(1)

        @pl.when(c == 1)
        def _():
            told(1)
            tell(2)

        @pl.when(c == 2)
        def _():
            told(2)

        message(c, 2).wait_recv()
        for cp in wcopy(c):
            cp.wait()

        @pl.when(c < CHUNKS - 1)
        def _():
            products(c, 0)

        @pl.when(c == CHUNKS - 1)
        def _():
            finish(0)

        @pl.when(c >= 2)
        def _():
            last_forwards(c - 2)

    def arrived(c):
        for m in (4, 7, 8, 9):
            message(c, m).wait_recv()

    def hidden_arrived(group):
        for n in range(NT):
            hcopy(group, n).wait_recv()

    in_gram(0)
    last_forwards(2)

    @pl.loop(0, CHUNKS - 1)
    def _(c):
        arrived(c)
        products(c, 1)

        @pl.when(c == 0)
        def _():
            hidden_arrived(0)
            take_rows(0, 0, 2 * HALF)
            last_forwards(3)

        @pl.when(c == 1)
        def _():
            gram(0, (0, 512), 0, 2 * HALF)

    arrived(CHUNKS - 1)
    finish(1)
    in_gram(1)
    in_sib = pltpu.make_async_remote_copy(
        src_ref=gin.at[pl.ds(256, 256), :], dst_ref=gin_sib, send_sem=in_s.at[0], recv_sem=in_r.at[0],
        device_id=sib, device_id_type=MESH,
    )
    in_sib.start()
    take_rows(1, 0, HALF)
    gram(1, (0, 256), 0, HALF)
    lane = lax.broadcasted_iota(I32, (16, 128), 1)

    def encode(halves, buf):
        codes = []
        for a, vals in enumerate(halves):
            q, code = row_code(vals)
            for b in range(8):
                buf[8 * a + b] = q[:, 128 * b:128 * b + 128]
            codes.append(code)
        buf[16] = jnp.where(lane < 64, codes[0], codes[1]).astype(I16)

    def decode(buf):
        codes = buf[16]
        out = []
        for a in range(2):
            s = row_scale(codes[:, 64 * a:64 * a + 1])
            cat = jnp.concatenate([buf[8 * a + b] for b in range(8)], axis=1)
            out.append(cat.astype(I32).astype(F32) * s)
        return out

    def g_halves(first):
        out = []
        for a in range(2):
            rows = pl.ds(pl.multiple_of(first + 16 * a, 16), 16)
            out.append(jnp.concatenate([g[n, rows, :] for n in range(NT)], axis=1))
        return out

    def ycopy(r):
        return pltpu.make_async_remote_copy(
            src_ref=ys.at[r], dst_ref=yr.at[r], send_sem=y_s.at[r], recv_sem=y_r.at[r],
            device_id=yfar, device_id_type=MESH,
        )

    def far(r):
        k = (r + 1) // 2
        return zpeer(jnp.where(r % 2 == 0, 4 + k, 4 - k))

    def fcopy(k):
        return pltpu.make_async_remote_copy(
            src_ref=fs.at[k], dst_ref=fr.at[k], send_sem=f_s.at[k], recv_sem=f_r.at[k],
            device_id=far(4 + k), device_id_type=MESH,
        )

    def zcopy(r):
        return pltpu.make_async_remote_copy(
            src_ref=zs.at[r], dst_ref=zr.at[r], send_sem=z_s.at[r], recv_sem=z_r.at[r],
            device_id=zpeer(STEP[r]), device_id_type=MESH,
        )

    def izcopy(r):
        return pltpu.make_async_remote_copy(
            src_ref=izs.at[r], dst_ref=izr.at[r], send_sem=iz_s.at[r], recv_sem=iz_r.at[r],
            device_id=far(r), device_id_type=MESH,
        )

    hidden_arrived(1)
    take_rows(1, HALF, HALF)
    gram(1, (0, 256), HALF, HALF)

    @pl.loop(0, 3)
    def _(k):
        encode(g_halves((4 + k) * 32), fs.at[k])
        fcopy(k).start()

    def y_send(r):
        encode(g_halves(r * 32), ys.at[r])
        ycopy(r).start()

    for r in (0, 2, 1):
        y_send(r)

    gram(1, (256, 256), 0, 2 * HALF)
    for r in (5, 6):
        encode(g_halves(256 + r * 32), zs.at[r])
        zcopy(r).start()

    def in_encode(vals, buf, at):
        top = jnp.max(jnp.max(jnp.abs(vals), axis=1, keepdims=True), axis=0, keepdims=True)
        code = jnp.ceil(8.0 * jnp.log2(jnp.maximum(top, 1e-30)))
        q = jnp.round(vals * (jnp.exp2(code * -0.125) * STEPS))
        q = jnp.where(irow == IN_ROWS, code, q).astype(I32).astype(I16)
        for b in range(3):
            buf[at, b] = q[:, 128 * b:128 * b + 128]

    def in_decode(buf, at):
        vals = jnp.concatenate([buf[at, b] for b in range(3)], axis=1).astype(I32).astype(F32)
        return vals * (jnp.exp2(vals[IN_ROWS:IN_ROWS + 1, 0:1] * 0.125) * (1.0 / STEPS))

    in_sib.wait_recv()
    gin[0:256, :] += gin_sib[...]

    @pl.loop(0, 8)
    def _(r):
        in_encode(gin[pl.ds(pl.multiple_of(16 * r, 16), 16), :], iys, r)

    in_y = pltpu.make_async_remote_copy(
        src_ref=iys, dst_ref=iyr, send_sem=in_s.at[1], recv_sem=in_r.at[1],
        device_id=yfar, device_id_type=MESH,
    )
    in_y.start()

    def add(xs, ys):
        return [a + b for a, b in zip(xs, ys)]

    y_send(3)

    def near(r):
        return g_halves(256 + r * 32)

    def from_y(r):
        ycopy(r).wait_recv()
        return decode(yr.at[r])

    def from_z(r):
        zcopy(r).wait_recv()
        return decode(zr.at[r])

    def z_send(r, vals):
        encode(vals, zs.at[r])
        zcopy(r).start()

    z_send(0, add(near(0), from_y(0)))
    z_send(2, add(near(2), from_y(2)))

    total = g_halves(7 * 32)
    for k in range(3):
        fcopy(k).wait_recv()
        total = add(total, decode(fr.at[k]))
    encode(total, ys.at[7])
    ycopy(7).start()

    z_send(1, add(add(near(1), from_y(1)), from_z(0)))
    z_send(4, add(near(4), from_z(2)))

    in_y.wait_recv()

    @pl.loop(0, 7)
    def _(r):
        rows = pl.ds(pl.multiple_of(128 + 16 * r, 16), 16)
        in_encode(gin[rows, :] + in_decode(iyr, r), izs, r)
        izcopy(r).start()

    z_send(3, add(near(3), from_y(3)))

    def put(vals):
        for a in range(2):
            oh_ref[pl.ds(16 * a, 16), :] = vals[a]

    total = near(7)
    for r in (5, 6):
        total = add(total, from_z(r))
    put(add(total, from_y(7)))
    total = in_decode(iyr, 7) + gin[pl.ds(128 + 16 * 7, 16), :]
    for r in range(7):
        izcopy(r).wait_recv()
        total += in_decode(izr, r)
    oin_ref[...] = total[:IN_ROWS] * INV
    total = [oh_ref[pl.ds(16 * a, 16), :] for a in range(2)]
    for r in (1, 4, 3):
        total = add(total, from_z(r))
    put([v * INV for v in total])

    @pl.loop(0, CHUNKS)
    def _(c):
        for m in range(NM):
            message(c, m).wait_send()

    for n in range(NT):
        hcopy(0, n).wait_send()
        hcopy(1, n).wait_send()

    for r in range(7):
        zcopy(r).wait_send()

    @pl.loop(0, 7)
    def _(r):
        izcopy(r).wait_send()

    for r in (0, 1, 2, 3, 7):
        ycopy(r).wait_send()
    for k in range(3):
        fcopy(k).wait_send()
    in_sib.wait_send()
    in_y.wait_send()


def pass_on(a_ref, b_ref, c_ref, d_ref):
    c_ref[...] = a_ref[...]
    d_ref[...] = b_ref[...]


def local(tokens, indices, gate_weight, up_weight):
    vmem = pltpu.VMEM
    dma = pltpu.SemaphoreType.DMA
    whole = pl.BlockSpec(memory_space=pl.ANY)
    out_shape = (
        jax.ShapeDtypeStruct((IN_ROWS, IBLK), F32),
        jax.ShapeDtypeStruct((OWN_ROWS, UNITS), F32),
    )
    factors = pl.pallas_call(
        kernel,
        out_shape=out_shape,
        in_specs=[whole] * 4,
        out_specs=[pl.BlockSpec(memory_space=vmem)] * 2,
        scratch_shapes=[
            vmem((1, SAMP), I32),
            vmem((SEQ, D), BF16),
            vmem((D, UNITS), BF16),
            vmem((D, UNITS), BF16),
            vmem((CHUNKS, ROWS, KC), BF16),
            vmem((NT, ROWS, TILE), F32),
            vmem((NT, ROWS, TILE), F32),
            vmem((2 * HALF, UNITS), BF16),
            vmem((2 * HALF, UNITS), BF16),
            vmem((512, 2 * HALF), BF16),
            vmem((512, 2 * HALF), BF16),
            vmem((NT, 512, TILE), F32),
            vmem((512, IBLK), BF16),
            vmem((512, IBLK), F32),
            vmem((256, IBLK), F32),
            vmem((8, 3, 16, 128), I16),
            vmem((8, 3, 16, 128), I16),
            vmem((7, 3, 16, 128), I16),
            vmem((7, 3, 16, 128), I16),
            vmem((8, 17, 16, 128), I16),
            vmem((8, 17, 16, 128), I16),
            vmem((3, 17, 16, 128), I16),
            vmem((3, 17, 16, 128), I16),
            vmem((7, 17, 16, 128), I16),
            vmem((7, 17, 16, 128), I16),
            dma((2,)),
            dma((CHUNKS, 2)),
            dma((CHUNKS, NM)),
            dma((CHUNKS, NM)),
            dma((2, NT)),
            dma((2, NT)),
            dma((8,)),
            dma((8,)),
            dma((3,)),
            dma((3,)),
            dma((7,)),
            dma((7,)),
            dma((2,)),
            dma((2,)),
            dma((7,)),
            dma((7,)),
            pltpu.SemaphoreType.REGULAR((3, 2)),
        ],
        compiler_params=pltpu.CompilerParams(
            collective_id=0, has_side_effects=True, vmem_limit_bytes=56 * 2**20
        ),
    )(indices.reshape(1, SAMP), tokens, gate_weight, up_weight)
    return pl.pallas_call(
        pass_on,
        out_shape=out_shape,
        in_specs=[pl.BlockSpec(memory_space=vmem)] * 2,
        out_specs=[pl.BlockSpec(memory_space=vmem)] * 2,
    )(*factors)


def solution(mesh):
    in_specs = (
        P(("dp", "tensor"), None),
        P(("dp", "tensor")),
        P(None, "tensor"),
        P(None, "tensor"),
    )
    out_specs = (P("dp", "tensor"), P("dp", "tensor"))
    return jax.shard_map(local, mesh=mesh, in_specs=in_specs, out_specs=out_specs, check_vma=False)
```

```python
import jax
import jax.numpy as jnp
from jax import lax
from jax.experimental import pallas as pl
from jax.experimental.pallas import tpu as pltpu
from jax.sharding import PartitionSpec as P

D = 3072
UNITS = 1024
IBLK = 384
SAMP = 64
SEQ = 128
ROWS = 512
CHUNKS = 4
KC = D // CHUNKS
TILE = 512
NT = UNITS // TILE
TURN = 256
OWN_ROWS = 32
IN_ROWS = 12
IN_PAD = 16
DZ = (4, 3, 5, 2, 6, 1, 7, 0)
STEP = (1, 3, 7, 2, 6, 1, 7)
INV = 1.0 / 16384
STEPS = 32000.0
MESH = pl.DeviceIdType.MESH
F32 = jnp.float32
BF16 = jnp.bfloat16
I16 = jnp.int16
I32 = jnp.int32

S_OWN, S_XM, S_XP, S_Y, S_YXM, S_YXP, S_X2, S_YX2 = (64 * i for i in range(8))
HALF = 256
MSGS = (
    (S_OWN, S_XM, 0, 64, "xp"),
    (S_OWN, S_XP, 0, 64, "xm"),
    (S_OWN, S_Y, 0, 64, "y"),
    (S_XM, S_X2, 0, 32, "xp"),
    (S_XP, S_X2, 32, 32, "xm"),
    (S_XM, S_YXM, 0, 64, "y"),
    (S_XP, S_YXP, 0, 64, "y"),
    (S_X2, S_YX2, 0, 32, "y"),
    (S_YXM, S_YX2, 32, 16, "xp"),
    (S_YXP, S_YX2, 48, 16, "xm"),
)
ARRIVAL = (0, 1, 2, 3, 6, 4, 5, 6, 6, 6)
LAST_ROWS = (S_X2 + 32, 96)
SENT_ROWS = sum(msg[3] for msg in MSGS)


def row_code(vals):
    top = jnp.max(jnp.abs(vals), axis=1, keepdims=True)
    code = jnp.ceil(8.0 * jnp.log2(jnp.maximum(top, 1e-30)))
    q = jnp.round(vals * (jnp.exp2(code * -0.125) * STEPS))
    return q.astype(I32).astype(I16), code.astype(I32)


def row_scale(code):
    return jnp.exp2(code.astype(I32).astype(F32) * 0.125) * (1.0 / STEPS)


def kernel(
    idx_hbm, tok_hbm, wg_hbm, wu_hbm, oin_ref, oh_ref,
    idx, tok, wg, wu, x, accg, accu, h1, h2, ht1, ht2, g, insel, gin, gin_sib,
    iys, iyr, izs, izr, ys, yr, fs, fr, zs, zr,
    tok_sem, w_sem, ag_s, ag_r, h_s, h_r, y_s, y_r, f_s, f_r, z_s, z_r, in_s, in_r, iz_s, iz_r, rel,
):
    dp = lax.axis_index("dp")
    t = lax.axis_index("tensor")
    yhi = dp // 16
    z = (dp // 2) % 8
    core = dp % 2
    xx = t // 2
    ylo = t % 2
    yhi_p = yhi + core * (1 - 2 * yhi)
    sib = (dp + 1 - 2 * core, t)
    ypart = (yhi_p * 16 + z * 2 + core, xx * 2 + 1 - ylo)
    yfar = (dp + 16 - 32 * yhi, t)
    where = {
        "xp": (dp, lax.rem(xx + 1, 4) * 2 + ylo),
        "xm": (dp, lax.rem(xx + 3, 4) * 2 + ylo),
        "y": ypart,
    }

    def zpeer(d):
        return (yhi * 16 + lax.rem(z + d, 8) * 2 + core, t)

    icopy = pltpu.make_async_copy(idx_hbm, idx, tok_sem.at[0])
    icopy.start()
    tcopy = pltpu.make_async_copy(tok_hbm, tok, tok_sem.at[1])
    tcopy.start()

    barrier = pltpu.get_barrier_semaphore()
    peers = [where["xp"], where["xm"], ypart, sib, yfar, zpeer(1), zpeer(7)]
    for peer in peers:
        pl.semaphore_signal(barrier, inc=1, device_id=peer, device_id_type=MESH)

    def wcopy(c):
        rows = pl.ds(pl.multiple_of(c * KC, KC), KC)
        return (
            pltpu.make_async_copy(wg_hbm.at[rows, :], wg.at[rows, :], w_sem.at[c, 0]),
            pltpu.make_async_copy(wu_hbm.at[rows, :], wu.at[rows, :], w_sem.at[c, 1]),
        )

    icopy.wait()
    pick = (lax.broadcasted_iota(I32, (SEQ, SAMP), 0) == idx[...]).astype(BF16)
    tcopy.wait()
    for c in range(CHUNKS):
        x[c, pl.ds(S_OWN, 64), :] = lax.dot_general(
            pick, tok[:, c * KC:(c + 1) * KC], (((0,), (0,)), ((), ())),
            preferred_element_type=F32,
        ).astype(BF16)
    for c in range(CHUNKS):
        for cp in wcopy(c):
            cp.start()

    pl.semaphore_wait(barrier, len(peers))

    def wait_for(ref, sem):
        pltpu.make_async_copy(ref, ref, sem).wait()

    def message(c, m):
        src, dst, first, n, way = MSGS[m]
        return pltpu.make_async_remote_copy(
            src_ref=x.at[c, pl.ds(src + first, n), :],
            dst_ref=x.at[c, pl.ds(dst + first, n), :],
            send_sem=ag_s.at[c],
            recv_sem=ag_r.at[c, ARRIVAL[m]],
            device_id=where[way],
            device_id_type=MESH,
        )

    def tell(k):
        pl.semaphore_signal(rel.at[k, 0], inc=1, device_id=zpeer(1), device_id_type=MESH)
        pl.semaphore_signal(rel.at[k, 1], inc=1, device_id=zpeer(7), device_id_type=MESH)

    def told(k):
        pl.semaphore_wait(rel.at[k, 0], 1)
        pl.semaphore_wait(rel.at[k, 1], 1)

    def forwards(c):
        message(c, 0).wait_recv()
        message(c, 3).start()
        message(c, 5).start()
        message(c, 1).wait_recv()
        message(c, 4).start()
        message(c, 6).start()

    def last_forwards(c):
        message(c, 3).wait_recv()
        message(c, 7).start()
        message(c, 5).wait_recv()
        message(c, 8).start()
        message(c, 6).wait_recv()
        message(c, 9).start()

    def products(c, group):
        mine = pl.ds(group * HALF, HALF)
        rows = pl.ds(pl.multiple_of(c * KC, KC), KC)

        @pl.loop(0, NT)
        def _(n):
            cols = pl.ds(pl.multiple_of(n * TILE, TILE), TILE)
            accg[n, mine, :] += jnp.dot(x[c, mine, :], wg[rows, cols], preferred_element_type=F32)
            accu[n, mine, :] += jnp.dot(x[c, mine, :], wu[rows, cols], preferred_element_type=F32)

    hidden = (h1, h2)
    turned = (ht1, ht2)

    def hcopy(group, n):
        ref = hidden[group]
        cols = pl.ds(pl.multiple_of(n * TILE, TILE), TILE)
        return pltpu.make_async_remote_copy(
            src_ref=ref.at[pl.ds(0, HALF), cols], dst_ref=ref.at[pl.ds(HALF, HALF), cols],
            send_sem=h_s.at[group, n], recv_sem=h_r.at[group, n],
            device_id=sib, device_id_type=MESH,
        )

    def finish(group):
        mine = pl.ds(group * HALF, HALF)
        rows = pl.ds((CHUNKS - 1) * KC, KC)

        @pl.loop(0, NT)
        def _(n):
            cols = pl.ds(pl.multiple_of(n * TILE, TILE), TILE)
            last = x[CHUNKS - 1, mine, :]
            gate = accg[n, mine, :] + jnp.dot(last, wg[rows, cols], preferred_element_type=F32)
            up = accu[n, mine, :] + jnp.dot(last, wu[rows, cols], preferred_element_type=F32)
            hidden[group][pl.ds(0, HALF), cols] = (gate / (1.0 + jnp.exp(-gate)) * up).astype(BF16)
            hcopy(group, n).start()

    scol = lax.broadcasted_iota(I32, (128, TURN), 1)
    srow = lax.broadcasted_iota(I32, (128, TURN), 0)
    pick_rows = (scol == (srow // 32) * 64 + core * 32 + srow % 32).astype(BF16)

    def take_rows(group, first, count):
        src = pl.ds(first, count)

        for n in range(UNITS // TURN):
            rows = lax.dot_general(
                pick_rows, hidden[group][src, n * TURN:(n + 1) * TURN], (((1,), (1,)), ((), ())),
                preferred_element_type=F32,
            ).astype(BF16)
            for q in range(4):
                dz = lax.rem((n % 2) * 4 + q + 8 - z, 8)
                place = jnp.where(dz >= 4, 2 * (dz - 4), 7 - 2 * dz)
                place = place + jnp.where(n // 2 == yhi, 8, 0)
                to = pl.ds(pl.multiple_of(place * 32, 32), 32)
                turned[group][to, src] = rows[q * 32:(q + 1) * 32]

    def gram(group, out, first, count):
        rows = pl.ds(out[0], out[1])
        src = pl.ds(first, count)

        @pl.loop(0, NT)
        def _(n):
            cols = pl.ds(pl.multiple_of(n * TILE, TILE), TILE)
            part = jnp.dot(turned[group][rows, src], hidden[group][src, cols], preferred_element_type=F32)
            if group == 0:
                g[n, rows, :] = part
            else:
                g[n, rows, :] += part

    for c in range(CHUNKS):
        for m in (0, 1, 2):
            message(c, m).start()
    tell(0)

    accg[...] = jnp.zeros_like(accg)
    accu[...] = jnp.zeros_like(accu)

    icol = lax.broadcasted_iota(I32, (IN_PAD, IBLK), 1)
    irow = lax.broadcasted_iota(I32, (IN_PAD, IBLK), 0)
    for r in range(32):
        to_y = (1 - yhi) if r % 16 < 8 else yhi
        to_core = core if r < 16 else 1 - core
        owner = to_y * 16 + lax.rem(z + DZ[r % 8], 8) * 2 + to_core
        block = (icol - owner * IN_ROWS == irow) & (irow < IN_ROWS)
        insel[pl.ds(r * IN_PAD, IN_PAD), :] = block.astype(BF16)

    def in_gram(group):
        xb = x[
            t // 2, pl.ds(group * HALF, HALF), pl.ds(pl.multiple_of((t % 2) * IBLK, IBLK), IBLK)
        ]
        xt = lax.dot_general(
            insel[...], xb, (((1,), (1,)), ((), ())), preferred_element_type=F32
        ).astype(BF16)
        part = jnp.dot(xt, xb, preferred_element_type=F32)
        if group == 0:
            gin[...] = part
        else:
            gin[...] += part

    @pl.loop(0, CHUNKS)
    def _(c):
        forwards(c)

        @pl.when(c == 0)
        def _():
            told(0)
            tell(1)

        @pl.when(c == 1)
        def _():
            told(1)
            tell(2)

        @pl.when(c == 2)
        def _():
            told(2)

        message(c, 2).wait_recv()
        for cp in wcopy(c):
            cp.wait()

        @pl.when(c < CHUNKS - 1)
        def _():
            products(c, 0)

        @pl.when(c == CHUNKS - 1)
        def _():
            finish(0)

        @pl.when(c >= 2)
        def _():
            last_forwards(c - 2)

    def arrived(c):
        wait_for(x.at[c, pl.ds(*LAST_ROWS), :], ag_r.at[c, 6])

    def hidden_arrived(group):
        for n in range(NT):
            hcopy(group, n).wait_recv()

    in_gram(0)
    last_forwards(2)

    @pl.loop(0, CHUNKS - 1)
    def _(c):
        arrived(c)
        products(c, 1)

        @pl.when(c == 0)
        def _():
            hidden_arrived(0)
            take_rows(0, 0, 2 * HALF)
            last_forwards(3)

        @pl.when(c == 1)
        def _():
            gram(0, (0, 512), 0, 2 * HALF)

    arrived(CHUNKS - 1)
    finish(1)
    in_gram(1)
    in_sib = pltpu.make_async_remote_copy(
        src_ref=gin.at[pl.ds(256, 256), :], dst_ref=gin_sib, send_sem=in_s.at[0], recv_sem=in_r.at[0],
        device_id=sib, device_id_type=MESH,
    )
    in_sib.start()
    take_rows(1, 0, HALF)
    gram(1, (0, 256), 0, HALF)
    lane = lax.broadcasted_iota(I32, (16, 128), 1)

    def encode(halves, buf):
        codes = []
        for a, vals in enumerate(halves):
            q, code = row_code(vals)
            for b in range(8):
                buf[8 * a + b] = q[:, 128 * b:128 * b + 128]
            codes.append(code)
        buf[16] = jnp.where(lane < 64, codes[0], codes[1]).astype(I16)

    def decode(buf):
        codes = buf[16]
        out = []
        for a in range(2):
            s = row_scale(codes[:, 64 * a:64 * a + 1])
            cat = jnp.concatenate([buf[8 * a + b] for b in range(8)], axis=1)
            out.append(cat.astype(I32).astype(F32) * s)
        return out

    def g_halves(first):
        out = []
        for a in range(2):
            rows = pl.ds(pl.multiple_of(first + 16 * a, 16), 16)
            out.append(jnp.concatenate([g[n, rows, :] for n in range(NT)], axis=1))
        return out

    def ycopy(r):
        return pltpu.make_async_remote_copy(
            src_ref=ys.at[r], dst_ref=yr.at[r], send_sem=y_s, recv_sem=y_r.at[r],
            device_id=yfar, device_id_type=MESH,
        )

    def far(r):
        k = (r + 1) // 2
        return zpeer(jnp.where(r % 2 == 0, 4 + k, 4 - k))

    def fcopy(k):
        return pltpu.make_async_remote_copy(
            src_ref=fs.at[k], dst_ref=fr.at[k], send_sem=f_s, recv_sem=f_r,
            device_id=far(4 + k), device_id_type=MESH,
        )

    def zcopy(r):
        return pltpu.make_async_remote_copy(
            src_ref=zs.at[r], dst_ref=zr.at[r], send_sem=z_s, recv_sem=z_r.at[r],
            device_id=zpeer(STEP[r]), device_id_type=MESH,
        )

    def izcopy(r):
        return pltpu.make_async_remote_copy(
            src_ref=izs.at[r], dst_ref=izr.at[r], send_sem=iz_s, recv_sem=iz_r,
            device_id=far(r), device_id_type=MESH,
        )

    hidden_arrived(1)
    take_rows(1, HALF, HALF)
    gram(1, (0, 256), HALF, HALF)

    @pl.loop(0, 3)
    def _(k):
        encode(g_halves((4 + k) * 32), fs.at[k])
        fcopy(k).start()

    def y_send(r):
        encode(g_halves(r * 32), ys.at[r])
        ycopy(r).start()

    for r in (0, 2, 1):
        y_send(r)

    gram(1, (256, 256), 0, 2 * HALF)
    for r in (5, 6):
        encode(g_halves(256 + r * 32), zs.at[r])
        zcopy(r).start()

    def in_encode(vals, buf, at):
        top = jnp.max(jnp.max(jnp.abs(vals), axis=1, keepdims=True), axis=0, keepdims=True)
        code = jnp.ceil(8.0 * jnp.log2(jnp.maximum(top, 1e-30)))
        q = jnp.round(vals * (jnp.exp2(code * -0.125) * STEPS))
        q = jnp.where(irow == IN_ROWS, code, q).astype(I32).astype(I16)
        for b in range(3):
            buf[at, b] = q[:, 128 * b:128 * b + 128]

    def in_decode(buf, at):
        vals = jnp.concatenate([buf[at, b] for b in range(3)], axis=1).astype(I32).astype(F32)
        return vals * (jnp.exp2(vals[IN_ROWS:IN_ROWS + 1, 0:1] * 0.125) * (1.0 / STEPS))

    in_sib.wait_recv()
    gin[0:256, :] += gin_sib[...]

    @pl.loop(0, 8)
    def _(r):
        in_encode(gin[pl.ds(pl.multiple_of(16 * r, 16), 16), :], iys, r)

    in_y = pltpu.make_async_remote_copy(
        src_ref=iys, dst_ref=iyr, send_sem=in_s.at[1], recv_sem=in_r.at[1],
        device_id=yfar, device_id_type=MESH,
    )
    in_y.start()

    def add(xs, ys):
        return [a + b for a, b in zip(xs, ys)]

    y_send(3)

    def near(r):
        return g_halves(256 + r * 32)

    def from_y(r):
        ycopy(r).wait_recv()
        return decode(yr.at[r])

    def from_z(r):
        zcopy(r).wait_recv()
        return decode(zr.at[r])

    def z_send(r, vals):
        encode(vals, zs.at[r])
        zcopy(r).start()

    @pl.loop(0, CHUNKS)
    def _(c):
        wait_for(x.at[c, pl.ds(0, SENT_ROWS), :], ag_s.at[c])

    for n in range(NT):
        hcopy(0, n).wait_send()
        hcopy(1, n).wait_send()

    z_send(0, add(near(0), from_y(0)))
    z_send(2, add(near(2), from_y(2)))

    total = g_halves(7 * 32)
    wait_for(fr, f_r)
    for k in range(3):
        total = add(total, decode(fr.at[k]))
    encode(total, ys.at[7])
    ycopy(7).start()

    z_send(1, add(add(near(1), from_y(1)), from_z(0)))
    z_send(4, add(near(4), from_z(2)))

    in_y.wait_recv()

    @pl.loop(0, 7)
    def _(r):
        rows = pl.ds(pl.multiple_of(128 + 16 * r, 16), 16)
        in_encode(gin[rows, :] + in_decode(iyr, r), izs, r)
        izcopy(r).start()

    z_send(3, add(near(3), from_y(3)))

    def put(vals):
        for a in range(2):
            oh_ref[pl.ds(16 * a, 16), :] = vals[a]

    total = near(7)
    for r in (5, 6):
        total = add(total, from_z(r))
    put(add(total, from_y(7)))
    total = in_decode(iyr, 7) + gin[pl.ds(128 + 16 * 7, 16), :]
    wait_for(izr, iz_r)
    for r in range(7):
        total += in_decode(izr, r)
    oin_ref[...] = total[:IN_ROWS] * INV
    total = [oh_ref[pl.ds(16 * a, 16), :] for a in range(2)]
    for r in (1, 4, 3):
        total = add(total, from_z(r))
    put([v * INV for v in total])

    wait_for(zs, z_s)
    wait_for(izs, iz_s)
    wait_for(ys.at[pl.ds(0, 5)], y_s)
    wait_for(fs, f_s)
    in_sib.wait_send()
    in_y.wait_send()


def pass_on(a_ref, b_ref, c_ref, d_ref):
    c_ref[...] = a_ref[...]
    d_ref[...] = b_ref[...]


def local(tokens, indices, gate_weight, up_weight):
    vmem = pltpu.VMEM
    dma = pltpu.SemaphoreType.DMA
    whole = pl.BlockSpec(memory_space=pl.ANY)
    out_shape = (
        jax.ShapeDtypeStruct((IN_ROWS, IBLK), F32),
        jax.ShapeDtypeStruct((OWN_ROWS, UNITS), F32),
    )
    factors = pl.pallas_call(
        kernel,
        out_shape=out_shape,
        in_specs=[whole] * 4,
        out_specs=[pl.BlockSpec(memory_space=vmem)] * 2,
        scratch_shapes=[
            vmem((1, SAMP), I32),
            vmem((SEQ, D), BF16),
            vmem((D, UNITS), BF16),
            vmem((D, UNITS), BF16),
            vmem((CHUNKS, ROWS, KC), BF16),
            vmem((NT, ROWS, TILE), F32),
            vmem((NT, ROWS, TILE), F32),
            vmem((2 * HALF, UNITS), BF16),
            vmem((2 * HALF, UNITS), BF16),
            vmem((512, 2 * HALF), BF16),
            vmem((512, 2 * HALF), BF16),
            vmem((NT, 512, TILE), F32),
            vmem((512, IBLK), BF16),
            vmem((512, IBLK), F32),
            vmem((256, IBLK), F32),
            vmem((8, 3, 16, 128), I16),
            vmem((8, 3, 16, 128), I16),
            vmem((7, 3, 16, 128), I16),
            vmem((7, 3, 16, 128), I16),
            vmem((8, 17, 16, 128), I16),
            vmem((8, 17, 16, 128), I16),
            vmem((3, 17, 16, 128), I16),
            vmem((3, 17, 16, 128), I16),
            vmem((7, 17, 16, 128), I16),
            vmem((7, 17, 16, 128), I16),
            dma((2,)),
            dma((CHUNKS, 2)),
            dma((CHUNKS,)),
            dma((CHUNKS, 7)),
            dma((2, NT)),
            dma((2, NT)),
            dma,
            dma((8,)),
            dma,
            dma,
            dma,
            dma((7,)),
            dma((2,)),
            dma((2,)),
            dma,
            dma,
            pltpu.SemaphoreType.REGULAR((3, 2)),
        ],
        compiler_params=pltpu.CompilerParams(
            collective_id=0, has_side_effects=True, vmem_limit_bytes=56 * 2**20
        ),
    )(indices.reshape(1, SAMP), tokens, gate_weight, up_weight)
    return pl.pallas_call(
        pass_on,
        out_shape=out_shape,
        in_specs=[pl.BlockSpec(memory_space=vmem)] * 2,
        out_specs=[pl.BlockSpec(memory_space=vmem)] * 2,
    )(*factors)


def solution(mesh):
    in_specs = (
        P(("dp", "tensor"), None),
        P(("dp", "tensor")),
        P(None, "tensor"),
        P(None, "tensor"),
    )
    out_specs = (P("dp", "tensor"), P("dp", "tensor"))
    return jax.shard_map(local, mesh=mesh, in_specs=in_specs, out_specs=out_specs, check_vma=False)
```

```python
import jax
import jax.numpy as jnp
from jax import lax
from jax.experimental import pallas as pl
from jax.experimental.pallas import tpu as pltpu
from jax.sharding import PartitionSpec as P

D = 3072
UNITS = 1024
IBLK = 384
SAMP = 64
SEQ = 128
ROWS = 512
CHUNKS = 4
KC = D // CHUNKS
TILE = 512
NT = UNITS // TILE
TURN = 256
OWN_ROWS = 32
IN_ROWS = 12
IN_PAD = 16
DZ = (4, 3, 5, 2, 6, 1, 7, 0)
STEP = (1, 3, 7, 2, 6, 1, 7)
INV = 1.0 / 16384
STEPS = 32000.0
MESH = pl.DeviceIdType.MESH
F32 = jnp.float32
BF16 = jnp.bfloat16
I16 = jnp.int16
I32 = jnp.int32

S_OWN, S_XM, S_XP, S_Y, S_YXM, S_YXP, S_X2, S_YX2 = (64 * i for i in range(8))
HALF = 256
MSGS = (
    (S_OWN, S_XM, 0, 64, "xp"),
    (S_OWN, S_XP, 0, 64, "xm"),
    (S_OWN, S_Y, 0, 64, "y"),
    (S_XM, S_X2, 0, 32, "xp"),
    (S_XP, S_X2, 32, 32, "xm"),
    (S_XM, S_YXM, 0, 64, "y"),
    (S_XP, S_YXP, 0, 64, "y"),
    (S_X2, S_YX2, 0, 32, "y"),
    (S_YXM, S_YX2, 32, 16, "xp"),
    (S_YXP, S_YX2, 48, 16, "xm"),
)
ARRIVAL = (0, 1, 2, 3, 6, 4, 5, 6, 6, 6)
LAST_ROWS = (S_X2 + 32, 96)
SENT_ROWS = sum(msg[3] for msg in MSGS)


def row_code(vals):
    top = jnp.max(jnp.abs(vals), axis=1, keepdims=True)
    code = jnp.ceil(8.0 * jnp.log2(jnp.maximum(top, 1e-30)))
    q = jnp.round(vals * (jnp.exp2(code * -0.125) * STEPS))
    return q.astype(I32).astype(I16), code.astype(I32)


def row_scale(code):
    return jnp.exp2(code.astype(I32).astype(F32) * 0.125) * (1.0 / STEPS)


def kernel(
    idx_hbm, tok_hbm, wg_hbm, wu_hbm, oin_ref, oh_ref,
    idx, tok, wg, wu, x, accg, accu, h1, h2, ht1, ht2, g, insel, gin, gin_sib,
    iys, iyr, izs, izr, ys, yr, fs, fr, zs, zr,
    tok_sem, w_sem, ag_s, ag_r, h_s, h_r, y_s, y_r, f_s, f_r, z_s, z_r, in_s, in_r, iz_s, iz_r, rel,
):
    dp = lax.axis_index("dp")
    t = lax.axis_index("tensor")
    yhi = dp // 16
    z = (dp // 2) % 8
    core = dp % 2
    xx = t // 2
    ylo = t % 2
    yhi_p = yhi + core * (1 - 2 * yhi)
    sib = (dp + 1 - 2 * core, t)
    ypart = (yhi_p * 16 + z * 2 + core, xx * 2 + 1 - ylo)
    yfar = (dp + 16 - 32 * yhi, t)
    where = {
        "xp": (dp, lax.rem(xx + 1, 4) * 2 + ylo),
        "xm": (dp, lax.rem(xx + 3, 4) * 2 + ylo),
        "y": ypart,
    }

    def zpeer(d):
        return (yhi * 16 + lax.rem(z + d, 8) * 2 + core, t)

    icopy = pltpu.make_async_copy(idx_hbm, idx, tok_sem.at[0])
    icopy.start()
    tcopy = pltpu.make_async_copy(tok_hbm, tok, tok_sem.at[1])
    tcopy.start()

    barrier = pltpu.get_barrier_semaphore()
    peers = [where["xp"], where["xm"], ypart, sib, yfar, zpeer(1), zpeer(7)]
    for peer in peers:
        pl.semaphore_signal(barrier, inc=1, device_id=peer, device_id_type=MESH)

    def wcopy(c):
        rows = pl.ds(pl.multiple_of(c * KC, KC), KC)
        return (
            pltpu.make_async_copy(wg_hbm.at[rows, :], wg.at[rows, :], w_sem.at[c, 0]),
            pltpu.make_async_copy(wu_hbm.at[rows, :], wu.at[rows, :], w_sem.at[c, 1]),
        )

    icopy.wait()
    pick = (lax.broadcasted_iota(I32, (SEQ, SAMP), 0) == idx[...]).astype(BF16)
    tcopy.wait()
    for c in range(CHUNKS):
        x[c, pl.ds(S_OWN, 64), :] = lax.dot_general(
            pick, tok[:, c * KC:(c + 1) * KC], (((0,), (0,)), ((), ())),
            preferred_element_type=F32,
        ).astype(BF16)
    for c in range(CHUNKS):
        for cp in wcopy(c):
            cp.start()

    pl.semaphore_wait(barrier, len(peers))

    def wait_for(ref, sem):
        pltpu.make_async_copy(ref, ref, sem).wait()

    def message(c, m):
        src, dst, first, n, way = MSGS[m]
        return pltpu.make_async_remote_copy(
            src_ref=x.at[c, pl.ds(src + first, n), :],
            dst_ref=x.at[c, pl.ds(dst + first, n), :],
            send_sem=ag_s.at[c],
            recv_sem=ag_r.at[c, ARRIVAL[m]],
            device_id=where[way],
            device_id_type=MESH,
        )

    def tell(k):
        pl.semaphore_signal(rel.at[k, 0], inc=1, device_id=zpeer(1), device_id_type=MESH)
        pl.semaphore_signal(rel.at[k, 1], inc=1, device_id=zpeer(7), device_id_type=MESH)

    def told(k):
        pl.semaphore_wait(rel.at[k, 0], 1)
        pl.semaphore_wait(rel.at[k, 1], 1)

    def forwards(c):
        message(c, 0).wait_recv()
        message(c, 3).start()
        message(c, 5).start()
        message(c, 1).wait_recv()
        message(c, 4).start()
        message(c, 6).start()

    def last_forwards(c):
        message(c, 3).wait_recv()
        message(c, 7).start()
        message(c, 5).wait_recv()
        message(c, 8).start()
        message(c, 6).wait_recv()
        message(c, 9).start()

    def products(c, group):
        mine = pl.ds(group * HALF, HALF)
        rows = pl.ds(pl.multiple_of(c * KC, KC), KC)

        @pl.loop(0, NT)
        def _(n):
            cols = pl.ds(pl.multiple_of(n * TILE, TILE), TILE)
            accg[n, mine, :] += jnp.dot(x[c, mine, :], wg[rows, cols], preferred_element_type=F32)
            accu[n, mine, :] += jnp.dot(x[c, mine, :], wu[rows, cols], preferred_element_type=F32)

    hidden = (h1, h2)
    turned = (ht1, ht2)

    def hcopy(group, n):
        ref = hidden[group]
        cols = pl.ds(pl.multiple_of(n * TILE, TILE), TILE)
        return pltpu.make_async_remote_copy(
            src_ref=ref.at[pl.ds(0, HALF), cols], dst_ref=ref.at[pl.ds(HALF, HALF), cols],
            send_sem=h_s.at[group, n], recv_sem=h_r.at[group, n],
            device_id=sib, device_id_type=MESH,
        )

    def finish(group):
        mine = pl.ds(group * HALF, HALF)
        rows = pl.ds((CHUNKS - 1) * KC, KC)

        @pl.loop(0, NT)
        def _(n):
            cols = pl.ds(pl.multiple_of(n * TILE, TILE), TILE)
            last = x[CHUNKS - 1, mine, :]
            gate = accg[n, mine, :] + jnp.dot(last, wg[rows, cols], preferred_element_type=F32)
            up = accu[n, mine, :] + jnp.dot(last, wu[rows, cols], preferred_element_type=F32)
            hidden[group][pl.ds(0, HALF), cols] = (gate / (1.0 + jnp.exp(-gate)) * up).astype(BF16)
            hcopy(group, n).start()

    scol = lax.broadcasted_iota(I32, (128, TURN), 1)
    srow = lax.broadcasted_iota(I32, (128, TURN), 0)
    pick_rows = (scol == (srow // 32) * 64 + core * 32 + srow % 32).astype(BF16)

    def take_rows(group, first, count):
        src = pl.ds(first, count)

        for n in range(UNITS // TURN):
            rows = lax.dot_general(
                pick_rows, hidden[group][src, n * TURN:(n + 1) * TURN], (((1,), (1,)), ((), ())),
                preferred_element_type=F32,
            ).astype(BF16)
            for q in range(4):
                dz = lax.rem((n % 2) * 4 + q + 8 - z, 8)
                place = jnp.where(dz >= 4, 2 * (dz - 4), 7 - 2 * dz)
                place = place + jnp.where(n // 2 == yhi, 8, 0)
                to = pl.ds(pl.multiple_of(place * 32, 32), 32)
                turned[group][to, src] = rows[q * 32:(q + 1) * 32]

    def gram(group, out, first, count):
        rows = pl.ds(out[0], out[1])
        src = pl.ds(first, count)

        @pl.loop(0, NT)
        def _(n):
            cols = pl.ds(pl.multiple_of(n * TILE, TILE), TILE)
            part = jnp.dot(turned[group][rows, src], hidden[group][src, cols], preferred_element_type=F32)
            if group == 0:
                g[n, rows, :] = part
            else:
                g[n, rows, :] += part

    for c in range(CHUNKS):
        for m in (0, 1, 2):
            message(c, m).start()
    tell(0)

    accg[...] = jnp.zeros_like(accg)
    accu[...] = jnp.zeros_like(accu)

    icol = lax.broadcasted_iota(I32, (IN_PAD, IBLK), 1)
    irow = lax.broadcasted_iota(I32, (IN_PAD, IBLK), 0)
    for r in range(32):
        to_y = (1 - yhi) if r % 16 < 8 else yhi
        to_core = core if r < 16 else 1 - core
        owner = to_y * 16 + lax.rem(z + DZ[r % 8], 8) * 2 + to_core
        block = (icol - owner * IN_ROWS == irow) & (irow < IN_ROWS)
        insel[pl.ds(r * IN_PAD, IN_PAD), :] = block.astype(BF16)

    def in_gram(group):
        xb = x[
            t // 2, pl.ds(group * HALF, HALF), pl.ds(pl.multiple_of((t % 2) * IBLK, IBLK), IBLK)
        ]
        xt = lax.dot_general(
            insel[...], xb, (((1,), (1,)), ((), ())), preferred_element_type=F32
        ).astype(BF16)
        part = jnp.dot(xt, xb, preferred_element_type=F32)
        if group == 0:
            gin[...] = part
        else:
            gin[...] += part

    @pl.loop(0, CHUNKS)
    def _(c):
        forwards(c)

        @pl.when(c == 0)
        def _():
            told(0)
            tell(1)

        @pl.when(c == 1)
        def _():
            told(1)
            tell(2)

        @pl.when(c == 2)
        def _():
            told(2)

        message(c, 2).wait_recv()
        for cp in wcopy(c):
            cp.wait()

        @pl.when(c < CHUNKS - 1)
        def _():
            products(c, 0)

        @pl.when(c == CHUNKS - 1)
        def _():
            finish(0)

        @pl.when(c >= 2)
        def _():
            last_forwards(c - 2)

    def arrived(c):
        wait_for(x.at[c, pl.ds(*LAST_ROWS), :], ag_r.at[c, 6])

    def hidden_arrived(group):
        for n in range(NT):
            hcopy(group, n).wait_recv()

    in_gram(0)
    last_forwards(2)

    @pl.loop(0, CHUNKS - 1)
    def _(c):
        arrived(c)
        products(c, 1)

        @pl.when(c == 0)
        def _():
            hidden_arrived(0)
            take_rows(0, 0, 2 * HALF)
            last_forwards(3)

        @pl.when(c == 1)
        def _():
            gram(0, (0, 512), 0, 2 * HALF)

    arrived(CHUNKS - 1)
    finish(1)
    in_gram(1)
    in_sib = pltpu.make_async_remote_copy(
        src_ref=gin.at[pl.ds(256, 256), :], dst_ref=gin_sib, send_sem=in_s.at[0], recv_sem=in_r.at[0],
        device_id=sib, device_id_type=MESH,
    )
    in_sib.start()
    take_rows(1, 0, HALF)
    gram(1, (0, 256), 0, HALF)
    lane = lax.broadcasted_iota(I32, (16, 128), 1)

    def encode(halves, buf):
        codes = []
        for a, vals in enumerate(halves):
            q, code = row_code(vals)
            for b in range(8):
                buf[8 * a + b] = q[:, 128 * b:128 * b + 128]
            codes.append(code)
        buf[16] = jnp.where(lane < 64, codes[0], codes[1]).astype(I16)

    def decode(buf):
        codes = buf[16]
        out = []
        for a in range(2):
            s = row_scale(codes[:, 64 * a:64 * a + 1])
            cat = jnp.concatenate([buf[8 * a + b] for b in range(8)], axis=1)
            out.append(cat.astype(I32).astype(F32) * s)
        return out

    def g_halves(first):
        out = []
        for a in range(2):
            rows = pl.ds(pl.multiple_of(first + 16 * a, 16), 16)
            out.append(jnp.concatenate([g[n, rows, :] for n in range(NT)], axis=1))
        return out

    def ycopy(r):
        return pltpu.make_async_remote_copy(
            src_ref=ys.at[r], dst_ref=yr.at[r], send_sem=y_s, recv_sem=y_r.at[r],
            device_id=yfar, device_id_type=MESH,
        )

    def far(r):
        k = (r + 1) // 2
        return zpeer(jnp.where(r % 2 == 0, 4 + k, 4 - k))

    def fcopy(k):
        return pltpu.make_async_remote_copy(
            src_ref=fs.at[k], dst_ref=fr.at[k], send_sem=f_s, recv_sem=f_r,
            device_id=far(4 + k), device_id_type=MESH,
        )

    def zcopy(r):
        return pltpu.make_async_remote_copy(
            src_ref=zs.at[r], dst_ref=zr.at[r], send_sem=z_s, recv_sem=z_r.at[r],
            device_id=zpeer(STEP[r]), device_id_type=MESH,
        )

    def izcopy(r):
        return pltpu.make_async_remote_copy(
            src_ref=izs.at[r], dst_ref=izr.at[r], send_sem=iz_s, recv_sem=iz_r,
            device_id=far(r), device_id_type=MESH,
        )

    hidden_arrived(1)
    take_rows(1, HALF, HALF)
    def y_send(r):
        encode(g_halves(r * 32), ys.at[r])
        ycopy(r).start()

    gram(1, (0, 128), HALF, HALF)
    y_send(0)
    y_send(2)
    gram(1, (128, 128), HALF, HALF)

    @pl.loop(0, 3)
    def _(k):
        encode(g_halves((4 + k) * 32), fs.at[k])
        fcopy(k).start()

    y_send(1)

    gram(1, (256, 256), 0, 2 * HALF)
    for r in (5, 6):
        encode(g_halves(256 + r * 32), zs.at[r])
        zcopy(r).start()

    def in_encode(vals, buf, at):
        top = jnp.max(jnp.max(jnp.abs(vals), axis=1, keepdims=True), axis=0, keepdims=True)
        code = jnp.ceil(8.0 * jnp.log2(jnp.maximum(top, 1e-30)))
        q = jnp.round(vals * (jnp.exp2(code * -0.125) * STEPS))
        q = jnp.where(irow == IN_ROWS, code, q).astype(I32).astype(I16)
        for b in range(3):
            buf[at, b] = q[:, 128 * b:128 * b + 128]

    def in_decode(buf, at):
        vals = jnp.concatenate([buf[at, b] for b in range(3)], axis=1).astype(I32).astype(F32)
        return vals * (jnp.exp2(vals[IN_ROWS:IN_ROWS + 1, 0:1] * 0.125) * (1.0 / STEPS))

    in_sib.wait_recv()
    gin[0:256, :] += gin_sib[...]

    @pl.loop(0, 8)
    def _(r):
        in_encode(gin[pl.ds(pl.multiple_of(16 * r, 16), 16), :], iys, r)

    in_y = pltpu.make_async_remote_copy(
        src_ref=iys, dst_ref=iyr, send_sem=in_s.at[1], recv_sem=in_r.at[1],
        device_id=yfar, device_id_type=MESH,
    )
    in_y.start()

    def add(xs, ys):
        return [a + b for a, b in zip(xs, ys)]

    y_send(3)

    def near(r):
        return g_halves(256 + r * 32)

    def from_y(r):
        ycopy(r).wait_recv()
        return decode(yr.at[r])

    def from_z(r):
        zcopy(r).wait_recv()
        return decode(zr.at[r])

    def z_send(r, vals):
        encode(vals, zs.at[r])
        zcopy(r).start()

    @pl.loop(0, CHUNKS)
    def _(c):
        wait_for(x.at[c, pl.ds(0, SENT_ROWS), :], ag_s.at[c])

    for n in range(NT):
        hcopy(0, n).wait_send()
        hcopy(1, n).wait_send()

    z_send(0, add(near(0), from_y(0)))
    z_send(2, add(near(2), from_y(2)))

    total = g_halves(7 * 32)
    wait_for(fr, f_r)
    for k in range(3):
        total = add(total, decode(fr.at[k]))
    encode(total, ys.at[7])
    ycopy(7).start()

    z_send(1, add(add(near(1), from_y(1)), from_z(0)))
    z_send(4, add(near(4), from_z(2)))

    in_y.wait_recv()

    @pl.loop(0, 7)
    def _(r):
        rows = pl.ds(pl.multiple_of(128 + 16 * r, 16), 16)
        in_encode(gin[rows, :] + in_decode(iyr, r), izs, r)
        izcopy(r).start()

    z_send(3, add(near(3), from_y(3)))

    def put(vals):
        for a in range(2):
            oh_ref[pl.ds(16 * a, 16), :] = vals[a]

    total = near(7)
    for r in (5, 6):
        total = add(total, from_z(r))
    put(add(total, from_y(7)))
    total = in_decode(iyr, 7) + gin[pl.ds(128 + 16 * 7, 16), :]
    wait_for(izr, iz_r)
    for r in range(7):
        total += in_decode(izr, r)
    oin_ref[...] = total[:IN_ROWS] * INV
    total = [oh_ref[pl.ds(16 * a, 16), :] for a in range(2)]
    for r in (1, 4, 3):
        total = add(total, from_z(r))
    put([v * INV for v in total])

    wait_for(zs, z_s)
    wait_for(izs, iz_s)
    wait_for(ys.at[pl.ds(0, 5)], y_s)
    wait_for(fs, f_s)
    in_sib.wait_send()
    in_y.wait_send()


def pass_on(a_ref, b_ref, c_ref, d_ref):
    c_ref[...] = a_ref[...]
    d_ref[...] = b_ref[...]


def local(tokens, indices, gate_weight, up_weight):
    vmem = pltpu.VMEM
    dma = pltpu.SemaphoreType.DMA
    whole = pl.BlockSpec(memory_space=pl.ANY)
    out_shape = (
        jax.ShapeDtypeStruct((IN_ROWS, IBLK), F32),
        jax.ShapeDtypeStruct((OWN_ROWS, UNITS), F32),
    )
    factors = pl.pallas_call(
        kernel,
        out_shape=out_shape,
        in_specs=[whole] * 4,
        out_specs=[pl.BlockSpec(memory_space=vmem)] * 2,
        scratch_shapes=[
            vmem((1, SAMP), I32),
            vmem((SEQ, D), BF16),
            vmem((D, UNITS), BF16),
            vmem((D, UNITS), BF16),
            vmem((CHUNKS, ROWS, KC), BF16),
            vmem((NT, ROWS, TILE), F32),
            vmem((NT, ROWS, TILE), F32),
            vmem((2 * HALF, UNITS), BF16),
            vmem((2 * HALF, UNITS), BF16),
            vmem((512, 2 * HALF), BF16),
            vmem((512, 2 * HALF), BF16),
            vmem((NT, 512, TILE), F32),
            vmem((512, IBLK), BF16),
            vmem((512, IBLK), F32),
            vmem((256, IBLK), F32),
            vmem((8, 3, 16, 128), I16),
            vmem((8, 3, 16, 128), I16),
            vmem((7, 3, 16, 128), I16),
            vmem((7, 3, 16, 128), I16),
            vmem((8, 17, 16, 128), I16),
            vmem((8, 17, 16, 128), I16),
            vmem((3, 17, 16, 128), I16),
            vmem((3, 17, 16, 128), I16),
            vmem((7, 17, 16, 128), I16),
            vmem((7, 17, 16, 128), I16),
            dma((2,)),
            dma((CHUNKS, 2)),
            dma((CHUNKS,)),
            dma((CHUNKS, 7)),
            dma((2, NT)),
            dma((2, NT)),
            dma,
            dma((8,)),
            dma,
            dma,
            dma,
            dma((7,)),
            dma((2,)),
            dma((2,)),
            dma,
            dma,
            pltpu.SemaphoreType.REGULAR((3, 2)),
        ],
        compiler_params=pltpu.CompilerParams(
            collective_id=0, has_side_effects=True, vmem_limit_bytes=56 * 2**20
        ),
    )(indices.reshape(1, SAMP), tokens, gate_weight, up_weight)
    return pl.pallas_call(
        pass_on,
        out_shape=out_shape,
        in_specs=[pl.BlockSpec(memory_space=vmem)] * 2,
        out_specs=[pl.BlockSpec(memory_space=vmem)] * 2,
    )(*factors)


def solution(mesh):
    in_specs = (
        P(("dp", "tensor"), None),
        P(("dp", "tensor")),
        P(None, "tensor"),
        P(None, "tensor"),
    )
    out_specs = (P("dp", "tensor"), P("dp", "tensor"))
    return jax.shard_map(local, mesh=mesh, in_specs=in_specs, out_specs=out_specs, check_vma=False)
```

```python
import jax
import jax.numpy as jnp
from jax import lax
from jax.experimental import pallas as pl
from jax.experimental.pallas import tpu as pltpu
from jax.sharding import PartitionSpec as P

D = 3072
UNITS = 1024
IBLK = 384
SAMP = 64
SEQ = 128
ROWS = 512
CHUNKS = 4
KC = D // CHUNKS
TILE = 512
NT = UNITS // TILE
TURN = 256
OWN_ROWS = 32
IN_ROWS = 12
IN_PAD = 16
DZ = (4, 3, 5, 2, 6, 1, 7, 0)
STEP = (1, 3, 7, 2, 6, 1, 7)
INV = 1.0 / 16384
STEPS = 32000.0
MESH = pl.DeviceIdType.MESH
F32 = jnp.float32
BF16 = jnp.bfloat16
I16 = jnp.int16
I32 = jnp.int32

S_OWN, S_XM, S_XP, S_Y, S_YXM, S_YXP, S_X2, S_YX2 = (64 * i for i in range(8))
HALF = 256
MSGS = (
    (S_OWN, S_XM, 0, 64, "xp"),
    (S_OWN, S_XP, 0, 64, "xm"),
    (S_OWN, S_Y, 0, 64, "y"),
    (S_XM, S_X2, 0, 32, "xp"),
    (S_XP, S_X2, 32, 32, "xm"),
    (S_XM, S_YXM, 0, 64, "y"),
    (S_XP, S_YXP, 0, 64, "y"),
    (S_X2, S_YX2, 0, 32, "y"),
    (S_YXM, S_YX2, 32, 16, "xp"),
    (S_YXP, S_YX2, 48, 16, "xm"),
)
ARRIVAL = (0, 1, 2, 3, 6, 4, 5, 6, 6, 6)
LAST_ROWS = (S_X2 + 32, 96)
SENT_ROWS = sum(msg[3] for msg in MSGS)


def row_code(vals):
    top = jnp.max(jnp.abs(vals), axis=1, keepdims=True)
    code = jnp.ceil(8.0 * jnp.log2(jnp.maximum(top, 1e-30)))
    q = jnp.round(vals * (jnp.exp2(code * -0.125) * STEPS))
    return q.astype(I32).astype(I16), code.astype(I32)


def row_scale(code):
    return jnp.exp2(code.astype(I32).astype(F32) * 0.125) * (1.0 / STEPS)


def kernel(
    idx_hbm, tok_hbm, wg_hbm, wu_hbm, oin_ref, oh_ref,
    idx, tok, wg, wu, x, accg, accu, h1, h2, ht1, ht2, g, insel, gin, gin_sib,
    iys, iyr, izs, izr, ys, yr, fs, fr, zs, zr,
    tok_sem, w_sem, ag_s, ag_r, h_s, h_r, y_s, y_r, f_s, f_r, z_s, z_r, in_s, in_r, iz_s, iz_r, rel,
):
    dp = lax.axis_index("dp")
    t = lax.axis_index("tensor")
    yhi = dp // 16
    z = (dp // 2) % 8
    core = dp % 2
    xx = t // 2
    ylo = t % 2
    yhi_p = yhi + core * (1 - 2 * yhi)
    sib = (dp + 1 - 2 * core, t)
    ypart = (yhi_p * 16 + z * 2 + core, xx * 2 + 1 - ylo)
    yfar = (dp + 16 - 32 * yhi, t)
    where = {
        "xp": (dp, lax.rem(xx + 1, 4) * 2 + ylo),
        "xm": (dp, lax.rem(xx + 3, 4) * 2 + ylo),
        "y": ypart,
    }

    def zpeer(d):
        return (yhi * 16 + lax.rem(z + d, 8) * 2 + core, t)

    icopy = pltpu.make_async_copy(idx_hbm, idx, tok_sem.at[0])
    icopy.start()
    tcopy = pltpu.make_async_copy(tok_hbm, tok, tok_sem.at[1])
    tcopy.start()

    barrier = pltpu.get_barrier_semaphore()
    peers = [where["xp"], where["xm"], ypart, sib, yfar, zpeer(1), zpeer(7)]
    for peer in peers:
        pl.semaphore_signal(barrier, inc=1, device_id=peer, device_id_type=MESH)

    def wcopy(c):
        rows = pl.ds(pl.multiple_of(c * KC, KC), KC)
        return (
            pltpu.make_async_copy(wg_hbm.at[rows, :], wg.at[rows, :], w_sem.at[c, 0]),
            pltpu.make_async_copy(wu_hbm.at[rows, :], wu.at[rows, :], w_sem.at[c, 1]),
        )

    icopy.wait()
    pick = (lax.broadcasted_iota(I32, (SEQ, SAMP), 0) == idx[...]).astype(BF16)
    tcopy.wait()
    for c in range(CHUNKS):
        x[c, pl.ds(S_OWN, 64), :] = lax.dot_general(
            pick, tok[:, c * KC:(c + 1) * KC], (((0,), (0,)), ((), ())),
            preferred_element_type=F32,
        ).astype(BF16)
    for c in range(CHUNKS):
        for cp in wcopy(c):
            cp.start()

    pl.semaphore_wait(barrier, len(peers))

    def wait_for(ref, sem):
        pltpu.make_async_copy(ref, ref, sem).wait()

    def message(c, m):
        src, dst, first, n, way = MSGS[m]
        return pltpu.make_async_remote_copy(
            src_ref=x.at[c, pl.ds(src + first, n), :],
            dst_ref=x.at[c, pl.ds(dst + first, n), :],
            send_sem=ag_s.at[c],
            recv_sem=ag_r.at[c, ARRIVAL[m]],
            device_id=where[way],
            device_id_type=MESH,
        )

    def tell(k):
        pl.semaphore_signal(rel.at[k, 0], inc=1, device_id=zpeer(1), device_id_type=MESH)
        pl.semaphore_signal(rel.at[k, 1], inc=1, device_id=zpeer(7), device_id_type=MESH)

    def told(k):
        pl.semaphore_wait(rel.at[k, 0], 1)
        pl.semaphore_wait(rel.at[k, 1], 1)

    def forwards(c):
        message(c, 0).wait_recv()
        message(c, 3).start()
        message(c, 5).start()
        message(c, 1).wait_recv()
        message(c, 4).start()
        message(c, 6).start()

    def last_forwards(c):
        message(c, 3).wait_recv()
        message(c, 7).start()
        message(c, 5).wait_recv()
        message(c, 8).start()
        message(c, 6).wait_recv()
        message(c, 9).start()

    def products(c, group):
        mine = pl.ds(group * HALF, HALF)
        rows = pl.ds(pl.multiple_of(c * KC, KC), KC)

        @pl.loop(0, NT)
        def _(n):
            cols = pl.ds(pl.multiple_of(n * TILE, TILE), TILE)
            accg[n, mine, :] += jnp.dot(x[c, mine, :], wg[rows, cols], preferred_element_type=F32)
            accu[n, mine, :] += jnp.dot(x[c, mine, :], wu[rows, cols], preferred_element_type=F32)

    hidden = (h1, h2)
    turned = (ht1, ht2)

    def hcopy(group, n):
        ref = hidden[group]
        cols = pl.ds(pl.multiple_of(n * TILE, TILE), TILE)
        return pltpu.make_async_remote_copy(
            src_ref=ref.at[pl.ds(0, HALF), cols], dst_ref=ref.at[pl.ds(HALF, HALF), cols],
            send_sem=h_s.at[group, n], recv_sem=h_r.at[group, n],
            device_id=sib, device_id_type=MESH,
        )

    def finish(group):
        mine = pl.ds(group * HALF, HALF)
        rows = pl.ds((CHUNKS - 1) * KC, KC)

        @pl.loop(0, NT)
        def _(n):
            cols = pl.ds(pl.multiple_of(n * TILE, TILE), TILE)
            last = x[CHUNKS - 1, mine, :]
            gate = accg[n, mine, :] + jnp.dot(last, wg[rows, cols], preferred_element_type=F32)
            up = accu[n, mine, :] + jnp.dot(last, wu[rows, cols], preferred_element_type=F32)
            hidden[group][pl.ds(0, HALF), cols] = (gate / (1.0 + jnp.exp(-gate)) * up).astype(BF16)
            hcopy(group, n).start()

    scol = lax.broadcasted_iota(I32, (128, TURN), 1)
    srow = lax.broadcasted_iota(I32, (128, TURN), 0)
    pick_rows = (scol == (srow // 32) * 64 + core * 32 + srow % 32).astype(BF16)

    def take_rows(group, first, count):
        src = pl.ds(first, count)

        for n in range(UNITS // TURN):
            rows = lax.dot_general(
                pick_rows, hidden[group][src, n * TURN:(n + 1) * TURN], (((1,), (1,)), ((), ())),
                preferred_element_type=F32,
            ).astype(BF16)
            for q in range(4):
                dz = lax.rem((n % 2) * 4 + q + 8 - z, 8)
                place = jnp.where(dz >= 4, 2 * (dz - 4), 7 - 2 * dz)
                place = place + jnp.where(n // 2 == yhi, 8, 0)
                to = pl.ds(pl.multiple_of(place * 32, 32), 32)
                turned[group][to, src] = rows[q * 32:(q + 1) * 32]

    def gram(group, out, first, count):
        rows = pl.ds(out[0], out[1])
        src = pl.ds(first, count)

        @pl.loop(0, NT)
        def _(n):
            cols = pl.ds(pl.multiple_of(n * TILE, TILE), TILE)
            part = jnp.dot(turned[group][rows, src], hidden[group][src, cols], preferred_element_type=F32)
            if group == 0:
                g[n, rows, :] = part
            else:
                g[n, rows, :] += part

    for c in range(CHUNKS):
        for m in (0, 1, 2):
            message(c, m).start()
    tell(0)

    accg[...] = jnp.zeros_like(accg)
    accu[...] = jnp.zeros_like(accu)

    icol = lax.broadcasted_iota(I32, (IN_PAD, IBLK), 1)
    irow = lax.broadcasted_iota(I32, (IN_PAD, IBLK), 0)
    for r in range(32):
        to_y = (1 - yhi) if r % 16 < 8 else yhi
        to_core = core if r < 16 else 1 - core
        owner = to_y * 16 + lax.rem(z + DZ[r % 8], 8) * 2 + to_core
        block = (icol - owner * IN_ROWS == irow) & (irow < IN_ROWS)
        insel[pl.ds(r * IN_PAD, IN_PAD), :] = block.astype(BF16)

    def in_gram(group):
        xb = x[
            t // 2, pl.ds(group * HALF, HALF), pl.ds(pl.multiple_of((t % 2) * IBLK, IBLK), IBLK)
        ]
        xt = lax.dot_general(
            insel[...], xb, (((1,), (1,)), ((), ())), preferred_element_type=F32
        ).astype(BF16)
        part = jnp.dot(xt, xb, preferred_element_type=F32)
        if group == 0:
            gin[...] = part
        else:
            gin[...] += part

    @pl.loop(0, CHUNKS)
    def _(c):
        forwards(c)

        @pl.when(c == 0)
        def _():
            told(0)
            tell(1)

        @pl.when(c == 1)
        def _():
            told(1)
            tell(2)

        @pl.when(c == 2)
        def _():
            told(2)

        message(c, 2).wait_recv()
        for cp in wcopy(c):
            cp.wait()

        @pl.when(c < CHUNKS - 1)
        def _():
            products(c, 0)

        @pl.when(c == CHUNKS - 1)
        def _():
            finish(0)

        @pl.when(c >= 2)
        def _():
            last_forwards(c - 2)

    def arrived(c):
        wait_for(x.at[c, pl.ds(*LAST_ROWS), :], ag_r.at[c, 6])

    def hidden_arrived(group):
        for n in range(NT):
            hcopy(group, n).wait_recv()

    in_gram(0)
    last_forwards(2)

    @pl.loop(0, CHUNKS - 1)
    def _(c):
        arrived(c)
        products(c, 1)

        @pl.when(c == 0)
        def _():
            hidden_arrived(0)
            take_rows(0, 0, 2 * HALF)
            last_forwards(3)

        @pl.when(c == 1)
        def _():
            gram(0, (0, 512), 0, 2 * HALF)

    arrived(CHUNKS - 1)
    finish(1)
    in_gram(1)
    in_sib = pltpu.make_async_remote_copy(
        src_ref=gin.at[pl.ds(256, 256), :], dst_ref=gin_sib, send_sem=in_s.at[0], recv_sem=in_r.at[0],
        device_id=sib, device_id_type=MESH,
    )
    in_sib.start()
    take_rows(1, 0, HALF)
    gram(1, (0, 256), 0, HALF)
    lane = lax.broadcasted_iota(I32, (16, 128), 1)

    def encode(halves, buf):
        codes = []
        for a, vals in enumerate(halves):
            q, code = row_code(vals)
            for b in range(8):
                buf[8 * a + b] = q[:, 128 * b:128 * b + 128]
            codes.append(code)
        buf[16] = jnp.where(lane < 64, codes[0], codes[1]).astype(I16)

    def decode(buf):
        codes = buf[16]
        out = []
        for a in range(2):
            s = row_scale(codes[:, 64 * a:64 * a + 1])
            cat = jnp.concatenate([buf[8 * a + b] for b in range(8)], axis=1)
            out.append(cat.astype(I32).astype(F32) * s)
        return out

    def g_halves(first):
        out = []
        for a in range(2):
            rows = pl.ds(pl.multiple_of(first + 16 * a, 16), 16)
            out.append(jnp.concatenate([g[n, rows, :] for n in range(NT)], axis=1))
        return out

    def ycopy(r):
        return pltpu.make_async_remote_copy(
            src_ref=ys.at[r], dst_ref=yr.at[r], send_sem=y_s, recv_sem=y_r.at[r],
            device_id=yfar, device_id_type=MESH,
        )

    def far(r):
        k = (r + 1) // 2
        return zpeer(jnp.where(r % 2 == 0, 4 + k, 4 - k))

    def fcopy(k):
        return pltpu.make_async_remote_copy(
            src_ref=fs.at[k], dst_ref=fr.at[k], send_sem=f_s, recv_sem=f_r,
            device_id=far(4 + k), device_id_type=MESH,
        )

    def zcopy(r):
        return pltpu.make_async_remote_copy(
            src_ref=zs.at[r], dst_ref=zr.at[r], send_sem=z_s, recv_sem=z_r.at[r],
            device_id=zpeer(STEP[r]), device_id_type=MESH,
        )

    def izcopy(r):
        return pltpu.make_async_remote_copy(
            src_ref=izs.at[r], dst_ref=izr.at[r], send_sem=iz_s, recv_sem=iz_r,
            device_id=far(r), device_id_type=MESH,
        )

    hidden_arrived(1)
    take_rows(1, HALF, HALF)
    def y_send(r):
        encode(g_halves(r * 32), ys.at[r])
        ycopy(r).start()

    gram(1, (0, 128), HALF, HALF)
    y_send(0)
    y_send(2)
    gram(1, (128, 128), HALF, HALF)

    @pl.loop(0, 3)
    def _(k):
        encode(g_halves((4 + k) * 32), fs.at[k])
        fcopy(k).start()

    y_send(1)

    gram(1, (256, 256), 0, 2 * HALF)
    for r in (5, 6):
        encode(g_halves(256 + r * 32), zs.at[r])
        zcopy(r).start()

    def in_encode(vals, buf, at):
        top = jnp.max(jnp.max(jnp.abs(vals), axis=1, keepdims=True), axis=0, keepdims=True)
        code = jnp.ceil(8.0 * jnp.log2(jnp.maximum(top, 1e-30)))
        q = jnp.round(vals * (jnp.exp2(code * -0.125) * STEPS))
        q = jnp.where(irow == IN_ROWS, code, q).astype(I32).astype(I16)
        for b in range(3):
            buf[at, b] = q[:, 128 * b:128 * b + 128]

    def in_decode(buf, at):
        vals = jnp.concatenate([buf[at, b] for b in range(3)], axis=1).astype(I32).astype(F32)
        return vals * (jnp.exp2(vals[IN_ROWS:IN_ROWS + 1, 0:1] * 0.125) * (1.0 / STEPS))

    in_sib.wait_recv()
    gin[0:256, :] += gin_sib[...]

    @pl.loop(0, 8)
    def _(r):
        in_encode(gin[pl.ds(pl.multiple_of(16 * r, 16), 16), :], iys, r)

    in_y = pltpu.make_async_remote_copy(
        src_ref=iys, dst_ref=iyr, send_sem=in_s.at[1], recv_sem=in_r.at[1],
        device_id=yfar, device_id_type=MESH,
    )
    in_y.start()

    def add(xs, ys):
        return [a + b for a, b in zip(xs, ys)]

    y_send(3)

    def near(r):
        return g_halves(256 + r * 32)

    def from_y(r):
        ycopy(r).wait_recv()
        return decode(yr.at[r])

    def from_z(r):
        zcopy(r).wait_recv()
        return decode(zr.at[r])

    def z_send(r, vals):
        encode(vals, zs.at[r])
        zcopy(r).start()

    @pl.loop(0, CHUNKS)
    def _(c):
        wait_for(x.at[c, pl.ds(0, SENT_ROWS), :], ag_s.at[c])

    for n in range(NT):
        hcopy(0, n).wait_send()
        hcopy(1, n).wait_send()

    z_send(0, add(near(0), from_y(0)))
    z_send(2, add(near(2), from_y(2)))

    total = g_halves(7 * 32)
    wait_for(fr, f_r)
    for k in range(3):
        total = add(total, decode(fr.at[k]))
    encode(total, ys.at[7])
    ycopy(7).start()

    z_send(1, add(add(near(1), from_y(1)), from_z(0)))

    in_y.wait_recv()

    @pl.loop(0, 7)
    def _(r):
        rows = pl.ds(pl.multiple_of(128 + 16 * r, 16), 16)
        in_encode(gin[rows, :] + in_decode(iyr, r), izs, r)
        izcopy(r).start()

    z_send(4, add(near(4), from_z(2)))

    z_send(3, add(near(3), from_y(3)))

    def put(vals):
        for a in range(2):
            oh_ref[pl.ds(16 * a, 16), :] = vals[a]

    total = near(7)
    for r in (5, 6):
        total = add(total, from_z(r))
    put(add(total, from_y(7)))
    total = in_decode(iyr, 7) + gin[pl.ds(128 + 16 * 7, 16), :]
    wait_for(izr, iz_r)
    for r in range(7):
        total += in_decode(izr, r)
    oin_ref[...] = total[:IN_ROWS] * INV
    total = [oh_ref[pl.ds(16 * a, 16), :] for a in range(2)]
    for r in (1, 4, 3):
        total = add(total, from_z(r))
    put([v * INV for v in total])

    wait_for(zs, z_s)
    wait_for(izs, iz_s)
    wait_for(ys.at[pl.ds(0, 5)], y_s)
    wait_for(fs, f_s)
    in_sib.wait_send()
    in_y.wait_send()


def pass_on(a_ref, b_ref, c_ref, d_ref):
    c_ref[...] = a_ref[...]
    d_ref[...] = b_ref[...]


def local(tokens, indices, gate_weight, up_weight):
    vmem = pltpu.VMEM
    dma = pltpu.SemaphoreType.DMA
    whole = pl.BlockSpec(memory_space=pl.ANY)
    out_shape = (
        jax.ShapeDtypeStruct((IN_ROWS, IBLK), F32),
        jax.ShapeDtypeStruct((OWN_ROWS, UNITS), F32),
    )
    factors = pl.pallas_call(
        kernel,
        out_shape=out_shape,
        in_specs=[whole] * 4,
        out_specs=[pl.BlockSpec(memory_space=vmem)] * 2,
        scratch_shapes=[
            vmem((1, SAMP), I32),
            vmem((SEQ, D), BF16),
            vmem((D, UNITS), BF16),
            vmem((D, UNITS), BF16),
            vmem((CHUNKS, ROWS, KC), BF16),
            vmem((NT, ROWS, TILE), F32),
            vmem((NT, ROWS, TILE), F32),
            vmem((2 * HALF, UNITS), BF16),
            vmem((2 * HALF, UNITS), BF16),
            vmem((512, 2 * HALF), BF16),
            vmem((512, 2 * HALF), BF16),
            vmem((NT, 512, TILE), F32),
            vmem((512, IBLK), BF16),
            vmem((512, IBLK), F32),
            vmem((256, IBLK), F32),
            vmem((8, 3, 16, 128), I16),
            vmem((8, 3, 16, 128), I16),
            vmem((7, 3, 16, 128), I16),
            vmem((7, 3, 16, 128), I16),
            vmem((8, 17, 16, 128), I16),
            vmem((8, 17, 16, 128), I16),
            vmem((3, 17, 16, 128), I16),
            vmem((3, 17, 16, 128), I16),
            vmem((7, 17, 16, 128), I16),
            vmem((7, 17, 16, 128), I16),
            dma((2,)),
            dma((CHUNKS, 2)),
            dma((CHUNKS,)),
            dma((CHUNKS, 7)),
            dma((2, NT)),
            dma((2, NT)),
            dma,
            dma((8,)),
            dma,
            dma,
            dma,
            dma((7,)),
            dma((2,)),
            dma((2,)),
            dma,
            dma,
            pltpu.SemaphoreType.REGULAR((3, 2)),
        ],
        compiler_params=pltpu.CompilerParams(
            collective_id=0, has_side_effects=True, vmem_limit_bytes=56 * 2**20
        ),
    )(indices.reshape(1, SAMP), tokens, gate_weight, up_weight)
    return pl.pallas_call(
        pass_on,
        out_shape=out_shape,
        in_specs=[pl.BlockSpec(memory_space=vmem)] * 2,
        out_specs=[pl.BlockSpec(memory_space=vmem)] * 2,
    )(*factors)


def solution(mesh):
    in_specs = (
        P(("dp", "tensor"), None),
        P(("dp", "tensor")),
        P(None, "tensor"),
        P(None, "tensor"),
    )
    out_specs = (P("dp", "tensor"), P("dp", "tensor"))
    return jax.shard_map(local, mesh=mesh, in_specs=in_specs, out_specs=out_specs, check_vma=False)
```
